256 devices in a mesh: dp: 64 (over y, z, core), tensor: 4 (over x).
Axes of the slice: x: 4, y: 4, z: 8, core: 2. Of those that a mesh axis runs over, the one named last changes fastest.
Arguments:
- gradient: bfloat16 [64, 128, 49152], P('dp', None, 'tensor'), may hold values from -12 to 12, as said below
- error_buffer: bfloat16 [64, 128, 49152], P('dp', None, 'tensor'), may hold values from -3 to 3
- q_prev: float32 [16, 49152], P(None, 'tensor'), may hold values from -6 to 6
Outputs:
- p_basis: float32 [128, 16], replicated
- q_new: float32 [16, 49152], P(None, 'tensor')
- residual: bfloat16 [64, 128, 49152], P('dp', None, 'tensor')
The draws below stay inside these ranges and needn't reach their ends.
Inputs may be any that keep to these rules, and one draw needn't show every extreme that they name: Each row of each replica's gradient carries its own scale, between 0.3 and 3.
All inputs are finite; a program needn't handle non-finite values.
Results may differ from the reference program's by a relative error of at most 0.001.
Values sent between devices are 32-bit elements; how exact they have to be, the bound alone decides.
A program may use at most 64 MiB of HBM per device.

```python
import math
import jax
import jax.numpy as jnp
from jax import lax

COLS = 49152
ROWS = 128
RANK = 16
REPLICAS = 64
N_DP = 64


def draw_gradient(key, part):
    key = jax.random.fold_in(key, 11)
    own_key, scale_key = jax.random.split(key, 2)
    own = jax.random.normal(own_key, (REPLICAS, ROWS, COLS), jnp.float32)
    scales = jnp.exp(jax.random.uniform(scale_key, (REPLICAS, ROWS, 1), jnp.float32, math.log(0.3), math.log(3.0)))
    mixed = own
    return jnp.clip(mixed * scales, -12.0, 12.0).astype(jnp.bfloat16)


def level_of(key, shape, cuts, smallest, top_value):
    gain, own = 1.0, jax.random.fold_in(key, 6)
    for axis_at, blocks in cuts:
        heights = jnp.exp(jax.random.uniform(jax.random.fold_in(own, axis_at), (blocks,), jnp.float32, smallest / len(cuts), top_value / len(cuts)))
        gain = gain * jnp.repeat(heights, shape[axis_at] // blocks).reshape([-1 if axis == axis_at else 1 for axis in range(len(shape))])
    return gain


def noise(rng, shape, spread, most, shards=(), held_as=jnp.bfloat16):
    array = spread * jax.random.normal(rng, shape, jnp.float32)
    if shards:
        array = array * level_of(rng, shape, shards, -0.22, 0.18)
    return jnp.clip(array, -most, most).astype(held_as)


def setup_inputs(seed: int = 0) -> dict:
    arg_keys = jax.random.split(jax.random.key(seed), 4)
    gradient = draw_gradient(jax.random.fold_in(arg_keys[3], 71), 0)
    error_buffer = noise(arg_keys[1], (REPLICAS, ROWS, COLS), 0.5, 3.0, ((0, 64), (2, 4)))
    q_prev = noise(arg_keys[2], (RANK, COLS), 1.0, 6.0, ((1, 4),), jnp.float32)
    return {"gradient": gradient, "error_buffer": error_buffer, "q_prev": q_prev}


PRECISE = lax.Precision.HIGHEST

def orthonormal(p_total):
    gram_matrix = jnp.dot(p_total.T, p_total, precision=PRECISE)
    factor = jnp.linalg.cholesky(gram_matrix)
    return jax.scipy.linalg.solve_triangular(factor, p_total.T, lower=True).T

def merged_rows(both_rows):
    return both_rows[0].astype(jnp.float32) + both_rows[1].astype(jnp.float32)

def reference(gradient, error_buffer, q_prev):

    def p_term(running, both_rows):
        merged = merged_rows(both_rows)
        return (running + lax.dot_general(merged, q_prev, (((1,), (1,)), ((), ())), precision=PRECISE), None)
    p_total, _ = lax.scan(p_term, jnp.zeros((ROWS, RANK), jnp.float32), (gradient, error_buffer))
    p_basis = orthonormal(p_total)

    def q_term(running, both_rows):
        merged = merged_rows(both_rows)
        return (running + lax.dot_general(p_basis, merged, (((0,), (0,)), ((), ())), precision=PRECISE), None)
    q_total, _ = lax.scan(q_term, jnp.zeros((RANK, COLS), jnp.float32), (gradient, error_buffer))
    q_new = q_total / N_DP
    update = jnp.dot(p_basis, q_new, precision=PRECISE)
    residual = lax.map(lambda both_rows: (merged_rows(both_rows) - update).astype(jnp.bfloat16), (gradient, error_buffer))
    return (p_basis, q_new, residual)
```

```python
import functools

import jax
import jax.numpy as jnp
from jax import lax
from jax.experimental import pallas as pl
from jax.experimental.pallas import tpu as pltpu
from jax.sharding import PartitionSpec as P

MESH = pl.DeviceIdType.MESH
F32 = jnp.float32
BF16 = jnp.bfloat16

NX, NY, NZ, NC = 4, 4, 8, 2
FAR = [4, 3, 5, 2, 6, 1, 7]
NEAR = FAR[::-1]
DYS = [2, 1, 3]


def position():
    dp, x = lax.axis_index("dp"), lax.axis_index("tensor")
    c = lax.rem(dp, NC)
    z = lax.rem(lax.div(dp, NC), NZ)
    y = lax.div(dp, NC * NZ)
    return x, y, z, c


def device(x, y, z, c):
    return ((y * NZ + z) * NC + c, x)


def parts_of(value, n):
    out = []
    for _ in range(n):
        part = value.astype(BF16)
        out.append(part)
        value = value - part.astype(F32)
    return out


def orthonormal_rows(pt):
    rank = pt.shape[0]
    gram = [
        jnp.broadcast_to(jnp.sum(pt * pt[k : k + 1], axis=1, keepdims=True), pt.shape)
        for k in range(rank)
    ]
    row = lax.broadcasted_iota(jnp.int32, pt.shape, 0)
    rows = []
    for k in range(rank):
        pivot = gram[k][k : k + 1]
        root = lax.rsqrt(pivot)
        root = root * (1.5 - 0.5 * pivot * root * root)
        factor = gram[k] * root
        basis = pt[k : k + 1] * root
        rows.append(basis)
        pt = pt - factor * basis
        for j in range(k + 1, rank):
            gram[j] = gram[j] - factor * factor[j : j + 1]
    del row
    return jnp.concatenate(rows, axis=0)


def reduce_kernel(
    g_hbm, e_hbm, q_hbm, pt_out, qn_out,
    ge, qprev, pcore, pz, pxy, psend, qloc, crecv, hs, yrecv, zs, zrecv, qn,
    load_sem, pc_sem, pz_sem, pxy_sem, c_sem, y_sem, z_sem, az_sem, ay_sem, ac_sem, out_sem,
):
    x, y, z, c = position()
    cols = q_hbm.shape[1]
    rows = g_hbm.shape[1]
    rank = q_hbm.shape[0]
    half = rank // NC
    unit = cols // (NY * NZ)
    group = NY * unit
    pending = []

    def send(src, dst, sems, index, to):
        copy = pltpu.make_async_remote_copy(
            src_ref=src, dst_ref=dst, send_sem=sems.at[(0,) + index], recv_sem=sems.at[(1,) + index],
            device_id=to, device_id_type=MESH,
        )
        copy.start()
        pending.append(copy)
        return copy

    loads = []
    for k in range(NZ):
        s = pl.ds(k * group, group)
        batch = [
            pltpu.make_async_copy(q_hbm.at[:, s], qprev.at[:, s], load_sem.at[k, 0]),
            pltpu.make_async_copy(g_hbm.at[0, :, s], ge.at[pl.ds(0, rows), s], load_sem.at[k, 1]),
            pltpu.make_async_copy(e_hbm.at[0, :, s], ge.at[pl.ds(rows, rows), s], load_sem.at[k, 2]),
        ]
        for copy in batch:
            copy.start()
        loads.append(batch)

    other = device(x, y, z, 1 - c)
    z_peer = {d: device(x, y, lax.rem(z + d, NZ), c) for d in range(1, NZ)}
    xy_peer = {
        (dx, dy): device(lax.rem(x + dx, NX), lax.rem(y + dy, NY), z, c)
        for dx in range(NX) for dy in range(NY) if (dx, dy) != (0, 0)
    }
    barrier = pltpu.get_barrier_semaphore()
    everyone = [other, *z_peer.values(), *xy_peer.values()]
    for peer in everyone:
        pl.semaphore_signal(barrier, inc=1, device_id=peer, device_id_type=MESH)

    total = jnp.zeros((3 * rank, 2 * rows), F32)
    for k in range(NZ):
        for copy in loads[k]:
            copy.wait()
        s = pl.ds(k * group, group)
        stack = jnp.concatenate(parts_of(qprev[:, s], 3), axis=0)
        total += lax.dot_general(stack, ge[:, s], (((1,), (1,)), ((), ())), preferred_element_type=F32)
    total = total[:, :rows] + total[:, rows:]
    mine = total[:rank] + total[rank : 2 * rank] + total[2 * rank :]

    pl.semaphore_wait(barrier, len(everyone))

    psend[0] = mine
    send(psend.at[0], pcore, pc_sem, (), other).wait_recv()
    mine = mine + pcore[...]
    psend[1] = mine
    pz[z] = mine
    copies = [send(psend.at[1], pz.at[z], pz_sem, (d,), z_peer[d]) for d in FAR]
    for copy in copies:
        copy.wait_recv()
    mine = pz[0]
    for k in range(1, NZ):
        mine = mine + pz[k]
    psend[2] = mine
    slot = y * NX + x
    pxy[slot] = mine
    order = sorted(xy_peer, key=lambda d: -(min(d[0], NX - d[0]) + min(d[1], NY - d[1])))
    copies = [send(psend.at[2], pxy.at[slot], pxy_sem, d, xy_peer[d]) for d in order]
    for copy in copies:
        copy.wait_recv()
    mine = pxy[0]
    for k in range(1, NX * NY):
        mine = mine + pxy[k]

    basis = orthonormal_rows(mine)
    pt_out[...] = basis
    stack = jnp.concatenate(parts_of(basis, 3), axis=0)
    stack = jnp.concatenate([stack, stack], axis=1)

    order = FAR + [0]
    copies = {}
    for d in order:
        s = pl.ds(pl.multiple_of(lax.rem(z + d, NZ) * group, group), group)
        three = jnp.dot(stack, ge[:, s], preferred_element_type=F32)
        local = three[:rank] + three[rank : 2 * rank] + three[2 * rank :]
        qloc[d, 0] = local[:half]
        qloc[d, 1] = local[half:]
        copies[d] = send(qloc.at[d, 1 - c], crecv.at[d], c_sem, (d,), other)
    y_copies = {}
    for d in order:
        copies[d].wait_recv()
        both = qloc[d, c] + crecv[d]
        for k in range(NY):
            hs[d, k] = both[:, k * unit : (k + 1) * unit]
        y_copies[d] = [
            send(hs.at[d, lax.rem(y + dy, NY)], yrecv.at[d, dy], y_sem, (d, dy), xy_peer[0, dy]) for dy in DYS
        ]
    z_copies = []
    for d in order:
        for copy in y_copies[d]:
            copy.wait_recv()
        value = hs[d, y] + yrecv[d, 1] + yrecv[d, 2] + yrecv[d, 3]
        if d:
            zs[d] = value
            z_copies.append(send(zs.at[d], zrecv.at[d], z_sem, (d,), z_peer[d]))
    for copy in z_copies:
        copy.wait_recv()
    for d in range(1, NZ):
        value = value + zrecv[d]
    value = value * (1.0 / (NY * NZ * NC))

    def place(ty, tz):
        return qn.at[c, :, pl.ds(pl.multiple_of(tz * group + ty * unit, 128), unit)]

    place(y, z)[...] = value
    z_copies = {d: send(place(y, z), place(y, z), az_sem, (d,), z_peer[d]) for d in FAR}
    y_copies = {}
    for d in [0] + NEAR:
        tz = lax.rem(z - d + NZ, NZ)
        if d:
            z_copies[d].wait_recv()
        y_copies[d] = [send(place(y, tz), place(y, tz), ay_sem, (d, dy), xy_peer[0, dy]) for dy in DYS]
    c_copies = {}
    for d in [0] + NEAR:
        for copy in y_copies[d]:
            copy.wait_recv()
        tz = lax.rem(z - d + NZ, NZ)
        span = qn.at[c, :, pl.ds(pl.multiple_of(tz * group, 128), group)]
        c_copies[d] = send(span, span, ac_sem, (d,), other)
    outs = []
    for d in [0] + NEAR:
        c_copies[d].wait_recv()
        tz = lax.rem(z - d + NZ, NZ)
        s = pl.ds(pl.multiple_of(tz * group, 128), group)
        copy = pltpu.make_async_copy(qn.at[:, :, s], qn_out.at[:, :, s], out_sem.at[d])
        copy.start()
        outs.append(copy)
    for copy in outs:
        copy.wait()
    for copy in pending:
        copy.wait_send()


def residual_kernel(pt_ref, q_ref, g_ref, e_ref, pt_out, q_out, r_out, pstack):
    @pl.when(pl.program_id(0) == 0)
    def _():
        pt_out[...] = pt_ref[...]
        p1, p2 = parts_of(pt_ref[...].T, 2)
        pstack[...] = jnp.concatenate([p1, p1, p2, p2], axis=1)

    q = q_ref[...]
    q_out[...] = q
    q1, q2 = parts_of(q, 2)
    update = jnp.dot(pstack[...], jnp.concatenate([q1, q2, q1, q2], axis=0), preferred_element_type=F32)
    merged = g_ref[0].astype(F32) + e_ref[0].astype(F32)
    r_out[0] = (merged - update).astype(BF16)


def shards(gradient, error_buffer, q_prev):
    _, rows, cols = gradient.shape
    rank = q_prev.shape[0]
    half = rank // NC
    unit = cols // (NY * NZ)
    group = NY * unit
    dma = pltpu.SemaphoreType.DMA
    vmem = pltpu.VMEM
    anywhere = pl.BlockSpec(memory_space=pl.ANY)
    pt, qn = pl.pallas_call(
        reduce_kernel,
        out_shape=(
            jax.ShapeDtypeStruct((rank, rows), F32),
            jax.ShapeDtypeStruct((NC, half, cols), F32),
        ),
        in_specs=[anywhere] * 3,
        out_specs=(pl.BlockSpec(memory_space=pltpu.VMEM), anywhere),
        scratch_shapes=[
            vmem((2 * rows, cols), BF16),
            vmem((rank, cols), F32),
            vmem((rank, rows), F32),
            vmem((NZ, rank, rows), F32),
            vmem((NX * NY, rank, rows), F32),
            vmem((3, rank, rows), F32),
            vmem((NZ, NC, half, group), F32),
            vmem((NZ, half, group), F32),
            vmem((NZ, NY, half, unit), F32),
            vmem((NZ, NY, half, unit), F32),
            vmem((NZ, half, unit), F32),
            vmem((NZ, half, unit), F32),
            vmem((NC, half, cols), F32),
            dma((NZ, 3)),
            dma((2,)),
            dma((2, NZ)),
            dma((2, NX, NY)),
            dma((2, NZ)),
            dma((2, NZ, NY)),
            dma((2, NZ)),
            dma((2, NZ)),
            dma((2, NZ, NY)),
            dma((2, NZ)),
            dma((NZ,)),
        ],
        compiler_params=pltpu.CompilerParams(
            collective_id=0, has_side_effects=True, vmem_limit_bytes=24 * 1024 * 1024
        ),
        cost_estimate=pl.CostEstimate(flops=2 * 10**8, bytes_accessed=8 * 10**6, transcendentals=0),
        name="reduce_factors",
    )(gradient, error_buffer, q_prev)
    qn = qn.reshape(rank, cols)

    block = cols // 8
    wide = pl.BlockSpec((1, rows, block), lambda i: (0, 0, i))
    tall = pl.BlockSpec((rank, block), lambda i: (0, i))
    whole = pl.BlockSpec((rank, rows), lambda i: (0, 0))
    pt, q_new, residual = pl.pallas_call(
        residual_kernel,
        grid=(cols // block,),
        out_shape=(
            jax.ShapeDtypeStruct((rank, rows), F32),
            jax.ShapeDtypeStruct((rank, cols), F32),
            jax.ShapeDtypeStruct((1, rows, cols), BF16),
        ),
        in_specs=[whole, tall, wide, wide],
        out_specs=(whole, tall, wide),
        scratch_shapes=[vmem((rows, 4 * rank), BF16)],
        compiler_params=pltpu.CompilerParams(vmem_limit_bytes=16 * 1024 * 1024),
        cost_estimate=pl.CostEstimate(flops=2 * 10**8, bytes_accessed=11 * 10**6, transcendentals=0),
        name="residual",
    )(pt, qn, gradient, error_buffer)
    return pt.T, q_new, residual


def solution(mesh):
    return jax.shard_map(
        shards,
        mesh=mesh,
        in_specs=(P("dp", None, "tensor"), P("dp", None, "tensor"), P(None, "tensor")),
        out_specs=(P(), P(None, "tensor"), P("dp", None, "tensor")),
        check_vma=False,
    )
```

```python
import functools

import jax
import jax.numpy as jnp
from jax import lax
from jax.experimental import pallas as pl
from jax.experimental.pallas import tpu as pltpu
from jax.sharding import PartitionSpec as P

MESH = pl.DeviceIdType.MESH
F32 = jnp.float32
BF16 = jnp.bfloat16

NX, NY, NZ, NC = 4, 4, 8, 2
FAR = [4, 3, 5, 2, 6, 1, 7]
NEAR = FAR[::-1]
DYS = [2, 1, 3]


def position():
    dp, x = lax.axis_index("dp"), lax.axis_index("tensor")
    c = lax.rem(dp, NC)
    z = lax.rem(lax.div(dp, NC), NZ)
    y = lax.div(dp, NC * NZ)
    return x, y, z, c


def device(x, y, z, c):
    return ((y * NZ + z) * NC + c, x)


def parts_of(value, n):
    out = []
    for _ in range(n):
        part = value.astype(BF16)
        out.append(part)
        value = value - part.astype(F32)
    return out


def orthonormal_rows(pt):
    rank = pt.shape[0]
    gram = [
        jnp.broadcast_to(jnp.sum(pt * pt[k : k + 1], axis=1, keepdims=True), pt.shape)
        for k in range(rank)
    ]
    row = lax.broadcasted_iota(jnp.int32, pt.shape, 0)
    rows = []
    for k in range(rank):
        pivot = gram[k][k : k + 1]
        root = lax.rsqrt(pivot)
        root = root * (1.5 - 0.5 * pivot * root * root)
        factor = gram[k] * root
        basis = pt[k : k + 1] * root
        rows.append(basis)
        pt = pt - factor * basis
        for j in range(k + 1, rank):
            gram[j] = gram[j] - factor * factor[j : j + 1]
    del row
    return jnp.concatenate(rows, axis=0)


def reduce_kernel(
    g_hbm, e_hbm, q_hbm, pt_out, qn, ge,
    qprev, pcore, pz, pxy, psend, qloc, crecv, hs, yrecv, zs, zrecv,
    load_sem, pc_sem, pz_sem, pxy_sem, c_sem, y_sem, z_sem, az_sem, ay_sem, ac_sem,
):
    x, y, z, c = position()
    cols = q_hbm.shape[1]
    rows = g_hbm.shape[1]
    rank = q_hbm.shape[0]
    half = rank // NC
    unit = cols // (NY * NZ)
    group = NY * unit
    pending = []

    def send(src, dst, sems, index, to):
        copy = pltpu.make_async_remote_copy(
            src_ref=src, dst_ref=dst, send_sem=sems.at[(0,) + index], recv_sem=sems.at[(1,) + index],
            device_id=to, device_id_type=MESH,
        )
        copy.start()
        pending.append(copy)
        return copy

    loads = []
    for k in range(NZ):
        s = pl.ds(k * group, group)
        batch = [
            pltpu.make_async_copy(q_hbm.at[:, s], qprev.at[:, s], load_sem.at[k, 0]),
            pltpu.make_async_copy(g_hbm.at[0, :, s], ge.at[pl.ds(0, rows), s], load_sem.at[k, 1]),
            pltpu.make_async_copy(e_hbm.at[0, :, s], ge.at[pl.ds(rows, rows), s], load_sem.at[k, 2]),
        ]
        for copy in batch:
            copy.start()
        loads.append(batch)

    other = device(x, y, z, 1 - c)
    z_peer = {d: device(x, y, lax.rem(z + d, NZ), c) for d in range(1, NZ)}
    xy_peer = {
        (dx, dy): device(lax.rem(x + dx, NX), lax.rem(y + dy, NY), z, c)
        for dx in range(NX) for dy in range(NY) if (dx, dy) != (0, 0)
    }
    barrier = pltpu.get_barrier_semaphore()
    everyone = [other, *z_peer.values(), *xy_peer.values()]
    for peer in everyone:
        pl.semaphore_signal(barrier, inc=1, device_id=peer, device_id_type=MESH)

    total = jnp.zeros((3 * rank, 2 * rows), F32)
    for k in range(NZ):
        for copy in loads[k]:
            copy.wait()
        s = pl.ds(k * group, group)
        stack = jnp.concatenate(parts_of(qprev[:, s], 3), axis=0)
        total += lax.dot_general(stack, ge[:, s], (((1,), (1,)), ((), ())), preferred_element_type=F32)
    total = total[:, :rows] + total[:, rows:]
    mine = total[:rank] + total[rank : 2 * rank] + total[2 * rank :]

    pl.semaphore_wait(barrier, len(everyone))

    psend[0] = mine
    send(psend.at[0], pcore, pc_sem, (), other).wait_recv()
    mine = mine + pcore[...]
    psend[1] = mine
    pz[z] = mine
    copies = [send(psend.at[1], pz.at[z], pz_sem, (d,), z_peer[d]) for d in FAR]
    for copy in copies:
        copy.wait_recv()
    mine = pz[0]
    for k in range(1, NZ):
        mine = mine + pz[k]
    psend[2] = mine
    slot = y * NX + x
    pxy[slot] = mine
    order = sorted(xy_peer, key=lambda d: -(min(d[0], NX - d[0]) + min(d[1], NY - d[1])))
    copies = [send(psend.at[2], pxy.at[slot], pxy_sem, d, xy_peer[d]) for d in order]
    for copy in copies:
        copy.wait_recv()
    mine = pxy[0]
    for k in range(1, NX * NY):
        mine = mine + pxy[k]

    basis = orthonormal_rows(mine)
    pt_out[...] = basis
    stack = jnp.concatenate(parts_of(basis, 3), axis=0)
    stack = jnp.concatenate([stack, stack], axis=1)

    order = FAR + [0]
    copies = {}
    for d in order:
        s = pl.ds(pl.multiple_of(lax.rem(z + d, NZ) * group, group), group)
        three = jnp.dot(stack, ge[:, s], preferred_element_type=F32)
        local = three[:rank] + three[rank : 2 * rank] + three[2 * rank :]
        qloc[d, 0] = local[:half]
        qloc[d, 1] = local[half:]
        copies[d] = send(qloc.at[d, 1 - c], crecv.at[d], c_sem, (d,), other)
    y_copies = {}
    for d in order:
        copies[d].wait_recv()
        both = qloc[d, c] + crecv[d]
        for k in range(NY):
            hs[d, k] = both[:, k * unit : (k + 1) * unit]
        y_copies[d] = [
            send(hs.at[d, lax.rem(y + dy, NY)], yrecv.at[d, dy], y_sem, (d, dy), xy_peer[0, dy]) for dy in DYS
        ]
    z_copies = []
    for d in order:
        for copy in y_copies[d]:
            copy.wait_recv()
        value = hs[d, y] + yrecv[d, 1] + yrecv[d, 2] + yrecv[d, 3]
        if d:
            zs[d] = value
            z_copies.append(send(zs.at[d], zrecv.at[d], z_sem, (d,), z_peer[d]))
    for copy in z_copies:
        copy.wait_recv()
    for d in range(1, NZ):
        value = value + zrecv[d]
    value = value * (1.0 / (NY * NZ * NC))

    def place(ty, tz):
        return qn.at[c, :, pl.ds(pl.multiple_of(tz * group + ty * unit, 128), unit)]

    place(y, z)[...] = value
    z_copies = {d: send(place(y, z), place(y, z), az_sem, (d,), z_peer[d]) for d in FAR}
    y_copies = {}
    for d in [0] + NEAR:
        tz = lax.rem(z - d + NZ, NZ)
        if d:
            z_copies[d].wait_recv()
        y_copies[d] = [send(place(y, tz), place(y, tz), ay_sem, (d, dy), xy_peer[0, dy]) for dy in DYS]
    c_copies = {}
    for d in [0] + NEAR:
        for copy in y_copies[d]:
            copy.wait_recv()
        tz = lax.rem(z - d + NZ, NZ)
        span = qn.at[c, :, pl.ds(pl.multiple_of(tz * group, 128), group)]
        c_copies[d] = send(span, span, ac_sem, (d,), other)
    for d in [0] + NEAR:
        c_copies[d].wait_recv()
    for copy in pending:
        copy.wait_send()


def residual_kernel(pt_ref, q_ref, ge, pt_out, q_out, r_out, held, sem, out_sem):
    rows, cols = held.shape
    rank = pt_ref.shape[0]
    block = cols // NZ
    copies = [
        pltpu.make_async_copy(q_ref, q_out, out_sem.at[0]),
        pltpu.make_async_copy(pt_ref, pt_out, out_sem.at[1]),
    ]
    for copy in copies:
        copy.start()
    p1, p2 = parts_of(pt_ref[...].T, 2)
    stack = jnp.concatenate([p1, p1, p2, p2], axis=1)
    for k in range(NZ):
        s = pl.ds(k * block, block)
        q1, q2 = parts_of(q_ref[:, :, s].reshape(rank, block), 2)
        update = jnp.dot(stack, jnp.concatenate([q1, q2, q1, q2], axis=0), preferred_element_type=F32)
        merged = ge[pl.ds(0, rows), s].astype(F32) + ge[pl.ds(rows, rows), s].astype(F32)
        held[:, s] = (merged - update).astype(BF16)
        copy = pltpu.make_async_copy(held.at[:, s], r_out.at[0, :, s], sem.at[k])
        copy.start()
        copies.append(copy)
    for copy in copies:
        copy.wait()


def shards(gradient, error_buffer, q_prev):
    _, rows, cols = gradient.shape
    rank = q_prev.shape[0]
    half = rank // NC
    unit = cols // (NY * NZ)
    group = NY * unit
    dma = pltpu.SemaphoreType.DMA
    vmem = pltpu.VMEM
    anywhere = pl.BlockSpec(memory_space=pl.ANY)
    inside = pl.BlockSpec(memory_space=pltpu.VMEM)
    pt, qn, ge = pl.pallas_call(
        reduce_kernel,
        out_shape=(
            vmem((rank, rows), F32),
            vmem((NC, half, cols), F32),
            vmem((2 * rows, cols), BF16),
        ),
        in_specs=[anywhere] * 3,
        out_specs=(inside,) * 3,
        scratch_shapes=[
            vmem((rank, cols), F32),
            vmem((rank, rows), F32),
            vmem((NZ, rank, rows), F32),
            vmem((NX * NY, rank, rows), F32),
            vmem((3, rank, rows), F32),
            vmem((NZ, NC, half, group), F32),
            vmem((NZ, half, group), F32),
            vmem((NZ, NY, half, unit), F32),
            vmem((NZ, NY, half, unit), F32),
            vmem((NZ, half, unit), F32),
            vmem((NZ, half, unit), F32),
            dma((NZ, 3)),
            dma((2,)),
            dma((2, NZ)),
            dma((2, NX, NY)),
            dma((2, NZ)),
            dma((2, NZ, NY)),
            dma((2, NZ)),
            dma((2, NZ)),
            dma((2, NZ, NY)),
            dma((2, NZ)),
        ],
        compiler_params=pltpu.CompilerParams(
            collective_id=0, has_side_effects=True, vmem_limit_bytes=24 * 1024 * 1024
        ),
        cost_estimate=pl.CostEstimate(flops=2 * 10**8, bytes_accessed=8 * 10**6, transcendentals=0),
        name="reduce_factors",
    )(*[pltpu.with_memory_space_constraint(v, pltpu.HBM) for v in (gradient, error_buffer, q_prev)])

    pt, q_new, residual = pl.pallas_call(
        residual_kernel,
        out_shape=(
            jax.ShapeDtypeStruct((rank, rows), F32),
            jax.ShapeDtypeStruct((NC, half, cols), F32),
            jax.ShapeDtypeStruct((1, rows, cols), BF16),
        ),
        in_specs=[inside] * 3,
        out_specs=(anywhere,) * 3,
        scratch_shapes=[vmem((rows, cols), BF16), dma((NZ,)), dma((2,))],
        compiler_params=pltpu.CompilerParams(vmem_limit_bytes=16 * 1024 * 1024),
        cost_estimate=pl.CostEstimate(flops=2 * 10**8, bytes_accessed=11 * 10**6, transcendentals=0),
        name="residual",
    )(pt, qn, ge)
    return pt.T, q_new.reshape(rank, cols), residual


def solution(mesh):
    return jax.shard_map(
        shards,
        mesh=mesh,
        in_specs=(P("dp", None, "tensor"), P("dp", None, "tensor"), P(None, "tensor")),
        out_specs=(P(), P(None, "tensor"), P("dp", None, "tensor")),
        check_vma=False,
    )
```

```python
import functools

import jax
import jax.numpy as jnp
from jax import lax
from jax.experimental import pallas as pl
from jax.experimental.pallas import tpu as pltpu
from jax.sharding import PartitionSpec as P

MESH = pl.DeviceIdType.MESH
F32 = jnp.float32
BF16 = jnp.bfloat16

NX, NY, NZ, NC = 4, 4, 8, 2
FAR = [4, 3, 5, 2, 6, 1, 7]
DIRECT = [1, 7, 0]
STAGED = [4, 3, 5, 2, 6]
DYS = [2, 1, 3]


def position():
    dp, x = lax.axis_index("dp"), lax.axis_index("tensor")
    c = lax.rem(dp, NC)
    z = lax.rem(lax.div(dp, NC), NZ)
    y = lax.div(dp, NC * NZ)
    return x, y, z, c


def device(x, y, z, c):
    return ((y * NZ + z) * NC + c, x)


def parts_of(value, n):
    out = []
    for _ in range(n):
        part = value.astype(BF16)
        out.append(part)
        value = value - part.astype(F32)
    return out


def orthonormal_rows(pt):
    rank = pt.shape[0]
    gram = [
        jnp.broadcast_to(jnp.sum(pt * pt[k : k + 1], axis=1, keepdims=True), pt.shape)
        for k in range(rank)
    ]
    rows = []
    for k in range(rank):
        pivot = gram[k][k : k + 1]
        root = lax.rsqrt(pivot)
        root = root * (1.5 - 0.5 * pivot * root * root)
        factor = gram[k] * root
        basis = pt[k : k + 1] * root
        rows.append(basis)
        pt = pt - factor * basis
        for j in range(k + 1, rank):
            gram[j] = gram[j] - factor * factor[j : j + 1]
    return jnp.concatenate(rows, axis=0)


def reduce_kernel(
    g_hbm, e_hbm, q_hbm, pt_out, qn, ge,
    qprev, psend, pz, pxy, msend, mrecv, mstack, hs, yrecv, zs, zrecv,
    load_sem, pz_sem, pxy_sem, m_sem, y_sem, z_sem, az_sem, ay_sem, ac_sem,
):
    x, y, z, c = position()
    cols = q_hbm.shape[1]
    rows = g_hbm.shape[1]
    rank = q_hbm.shape[0]
    half = rank // NC
    span = cols // NC
    group = span // NZ
    unit = group // 2
    pending = []

    def send(src, dst, sems, index, to):
        copy = pltpu.make_async_remote_copy(
            src_ref=src, dst_ref=dst, send_sem=sems.at[(0,) + index], recv_sem=sems.at[(1,) + index],
            device_id=to, device_id_type=MESH,
        )
        copy.start()
        pending.append(copy)
        return copy

    def peer(dx=0, dy=0, dz=0, dc=0):
        return device(
            lax.rem(x + dx, NX) if dx else x, lax.rem(y + dy, NY) if dy else y,
            lax.rem(z + dz, NZ) if dz else z, 1 - c if dc else c,
        )

    wide = cols // NZ
    loads = []
    for k in range(NZ):
        s = pl.ds(k * wide, wide)
        batch = [
            pltpu.make_async_copy(q_hbm.at[:, s], qprev.at[:, s], load_sem.at[k, 0]),
            pltpu.make_async_copy(g_hbm.at[0, :, s], ge.at[pl.ds(0, rows), s], load_sem.at[k, 1]),
            pltpu.make_async_copy(e_hbm.at[0, :, s], ge.at[pl.ds(rows, rows), s], load_sem.at[k, 2]),
        ]
        for copy in batch:
            copy.start()
        loads.append(batch)

    offsets = [(0, 0, dz, dc) for dz in range(NZ) for dc in range(NC)]
    offsets += [(dx, dy, 0, dc) for dx in range(NX) for dy in range(NY) for dc in range(NC)]
    offsets += [(0, dy, dz, 0) for dy in range(NY) for dz in DIRECT]
    offsets = [o for o in dict.fromkeys(offsets) if o != (0, 0, 0, 0)]
    barrier = pltpu.get_barrier_semaphore()
    for o in offsets:
        pl.semaphore_signal(barrier, inc=1, device_id=peer(*o), device_id_type=MESH)

    total = jnp.zeros((3 * rank, 2 * rows), F32)
    for k in range(NZ):
        for copy in loads[k]:
            copy.wait()
        s = pl.ds(k * wide, wide)
        stack = jnp.concatenate(parts_of(qprev[:, s], 3), axis=0)
        total += lax.dot_general(stack, ge[:, s], (((1,), (1,)), ((), ())), preferred_element_type=F32)
    total = total[:, :rows] + total[:, rows:]
    mine = total[:rank] + total[rank : 2 * rank] + total[2 * rank :]

    pl.semaphore_wait(barrier, len(offsets))

    psend[0] = mine[:half]
    psend[1] = mine[half:]
    slot = z * NC + c
    copies = []
    for d in FAR + [0]:
        if d:
            copies.append(send(psend.at[c], pz.at[slot], pz_sem, (d, 0), peer(dz=d)))
        copies.append(send(psend.at[1 - c], pz.at[slot], pz_sem, (d, 1), peer(dz=d, dc=1)))
    pz[slot] = psend[c]

    m_copies = []
    for k in range(NZ):
        s = pl.ds(pl.multiple_of((1 - c) * span + k * group, 128), group)
        msend[k] = ge[pl.ds(0, rows), s].astype(F32) + ge[pl.ds(rows, rows), s].astype(F32)
        m_copies.append(send(msend.at[k], mrecv.at[k], m_sem, (k,), peer(dc=1)))

    for copy in copies:
        copy.wait_recv()
    mine = pz[0]
    for k in range(1, NZ * NC):
        mine = mine + pz[k]

    psend[2] = mine
    slot = y * NX + x
    order = sorted(
        [(dx, dy) for dx in range(NX) for dy in range(NY)],
        key=lambda d: -(min(d[0], NX - d[0]) + min(d[1], NY - d[1])),
    )
    copies = []
    for dx, dy in order:
        if (dx, dy) != (0, 0):
            copies.append(send(psend.at[2], pxy.at[slot, c], pxy_sem, (dx, dy, 0), peer(dx, dy)))
        copies.append(send(psend.at[2], pxy.at[slot, c], pxy_sem, (dx, dy, 1), peer(dx, dy, dc=1)))
    pxy[slot, c] = mine

    for k in range(NZ):
        m_copies[k].wait_recv()
        s = pl.ds(pl.multiple_of(c * span + k * group, 128), group)
        both = ge[pl.ds(0, rows), s].astype(F32) + ge[pl.ds(rows, rows), s].astype(F32) + mrecv[k]
        for i, part in enumerate(parts_of(both, 3)):
            mstack[k, pl.ds(i * rows, rows)] = part

    for copy in copies:
        copy.wait_recv()
    mine = pxy[0]
    for k in range(1, NX * NY):
        mine = mine + pxy[k]

    basis = orthonormal_rows(mine.reshape(rank, rows))
    pt_out[...] = basis
    stack = jnp.concatenate(parts_of(basis, 3), axis=0)
    stack = jnp.concatenate([stack] * 3, axis=1)

    order = FAR + [0]
    y_copies = {}
    for d in order:
        three = jnp.dot(stack, mstack[lax.rem(z + d, NZ)], preferred_element_type=F32)
        local = three[:rank] + three[rank : 2 * rank] + three[2 * rank :]
        for k in range(NY):
            hs[d, k] = local[k // 2 * half : (k // 2 + 1) * half, k % 2 * unit : (k % 2 + 1) * unit]
        y_copies[d] = [
            send(hs.at[d, lax.rem(y + dy, NY)], yrecv.at[d, dy], y_sem, (d, dy), peer(dy=dy)) for dy in DYS
        ]
    z_copies = []
    for d in order:
        for copy in y_copies[d]:
            copy.wait_recv()
        value = hs[d, y] + yrecv[d, 1] + yrecv[d, 2] + yrecv[d, 3]
        if d:
            zs[d] = value
            z_copies.append(send(zs.at[d], zrecv.at[d], z_sem, (d,), peer(dz=d)))
    for copy in z_copies:
        copy.wait_recv()
    for d in range(1, NZ):
        value = value + zrecv[d]
    value = value * (1.0 / (NY * NZ * NC))

    def place(ty, tz):
        start = c * span + tz * group + lax.rem(ty, 2) * unit
        return qn.at[lax.div(ty, 2), :, pl.ds(pl.multiple_of(start, 128), unit)]

    def forward(d, dy):
        ref = place(lax.rem(y + NY - dy, NY), lax.rem(z + NZ - d, NZ))
        c_copies.append(send(ref, ref, ac_sem, (d, dy), peer(dc=1)))

    own = place(y, z)
    own[...] = value
    c_copies, y_copies, z_copies = [], {}, {}
    for d in STAGED:
        z_copies[d] = send(own, own, az_sem, (d,), peer(dz=d))
    for d in DIRECT:
        for dy in (2, 1, 3, 0):
            if d or dy:
                y_copies[d, dy] = send(own, own, ay_sem, (d, dy), peer(dy=dy, dz=d))
    forward(0, 0)
    for d in STAGED[::-1]:
        z_copies[d].wait_recv()
        ref = place(y, lax.rem(z + NZ - d, NZ))
        for dy in DYS:
            y_copies[d, dy] = send(ref, ref, ay_sem, (d, dy), peer(dy=dy))
        forward(d, 0)
    for d in DIRECT[::-1] + STAGED[::-1]:
        for dy in (0, 1, 3, 2):
            if (d, dy) in y_copies:
                y_copies[d, dy].wait_recv()
                forward(d, dy)
    for copy in c_copies:
        copy.wait_recv()
    for copy in pending:
        copy.wait_send()


def residual_kernel(pt_ref, q_ref, ge, pt_out, q_out, r_out, held, sem, out_sem):
    rows, cols = held.shape
    rank = pt_ref.shape[0]
    block = cols // NZ
    copies = [
        pltpu.make_async_copy(q_ref, q_out, out_sem.at[0]),
        pltpu.make_async_copy(pt_ref, pt_out, out_sem.at[1]),
    ]
    for copy in copies:
        copy.start()
    p1, p2 = parts_of(pt_ref[...].T, 2)
    stack = jnp.concatenate([p1, p1, p2, p2], axis=1)
    for k in range(NZ):
        s = pl.ds(k * block, block)
        q1, q2 = parts_of(q_ref[:, :, s].reshape(rank, block), 2)
        update = jnp.dot(stack, jnp.concatenate([q1, q2, q1, q2], axis=0), preferred_element_type=F32)
        merged = ge[pl.ds(0, rows), s].astype(F32) + ge[pl.ds(rows, rows), s].astype(F32)
        held[:, s] = (merged - update).astype(BF16)
        copy = pltpu.make_async_copy(held.at[:, s], r_out.at[0, :, s], sem.at[k])
        copy.start()
        copies.append(copy)
    for copy in copies:
        copy.wait()


def shards(gradient, error_buffer, q_prev):
    _, rows, cols = gradient.shape
    rank = q_prev.shape[0]
    half = rank // NC
    unit = cols // (NY * NZ)
    group = cols // NC // NZ
    dma = pltpu.SemaphoreType.DMA
    vmem = pltpu.VMEM
    anywhere = pl.BlockSpec(memory_space=pl.ANY)
    inside = pl.BlockSpec(memory_space=pltpu.VMEM)
    pt, qn, ge = pl.pallas_call(
        reduce_kernel,
        out_shape=(
            vmem((rank, rows), F32),
            vmem((NC, half, cols), F32),
            vmem((2 * rows, cols), BF16),
        ),
        in_specs=[anywhere] * 3,
        out_specs=(inside,) * 3,
        scratch_shapes=[
            vmem((rank, cols), F32),
            vmem((3, half, rows), F32),
            vmem((NZ * NC, half, rows), F32),
            vmem((NX * NY, NC, half, rows), F32),
            vmem((NZ, rows, group), F32),
            vmem((NZ, rows, group), F32),
            vmem((NZ, 3 * rows, group), BF16),
            vmem((NZ, NY, half, unit), F32),
            vmem((NZ, NY, half, unit), F32),
            vmem((NZ, half, unit), F32),
            vmem((NZ, half, unit), F32),
            dma((NZ, 3)),
            dma((2, NZ, NC)),
            dma((2, NX, NY, NC)),
            dma((2, NZ)),
            dma((2, NZ, NY)),
            dma((2, NZ)),
            dma((2, NZ)),
            dma((2, NZ, NY)),
            dma((2, NZ, NY)),
        ],
        compiler_params=pltpu.CompilerParams(
            collective_id=0, has_side_effects=True, vmem_limit_bytes=32 * 1024 * 1024
        ),
        cost_estimate=pl.CostEstimate(flops=2 * 10**8, bytes_accessed=8 * 10**6, transcendentals=0),
        name="reduce_factors",
    )(*[pltpu.with_memory_space_constraint(v, pltpu.HBM) for v in (gradient, error_buffer, q_prev)])

    pt, q_new, residual = pl.pallas_call(
        residual_kernel,
        out_shape=(
            jax.ShapeDtypeStruct((rank, rows), F32),
            jax.ShapeDtypeStruct((NC, half, cols), F32),
            jax.ShapeDtypeStruct((1, rows, cols), BF16),
        ),
        in_specs=[inside] * 3,
        out_specs=(anywhere,) * 3,
        scratch_shapes=[vmem((rows, cols), BF16), dma((NZ,)), dma((2,))],
        compiler_params=pltpu.CompilerParams(vmem_limit_bytes=16 * 1024 * 1024),
        cost_estimate=pl.CostEstimate(flops=2 * 10**8, bytes_accessed=11 * 10**6, transcendentals=0),
        name="residual",
    )(pt, qn, ge)
    return pt.T, q_new.reshape(rank, cols), residual


def solution(mesh):
    return jax.shard_map(
        shards,
        mesh=mesh,
        in_specs=(P("dp", None, "tensor"), P("dp", None, "tensor"), P(None, "tensor")),
        out_specs=(P(), P(None, "tensor"), P("dp", None, "tensor")),
        check_vma=False,
    )
```

```python
import functools

import jax
import jax.numpy as jnp
from jax import lax
from jax.experimental import pallas as pl
from jax.experimental.pallas import tpu as pltpu
from jax.sharding import PartitionSpec as P

MESH = pl.DeviceIdType.MESH
F32 = jnp.float32
BF16 = jnp.bfloat16

NX, NY, NZ, NC = 4, 4, 8, 2
FAR = [4, 3, 5, 2, 6, 1, 7]
DIRECT = [1, 7, 0]
STAGED = [4, 3, 5, 2, 6]
DYS = [2, 1, 3]
LAST = 4
LOADS = 6


def position():
    dp, x = lax.axis_index("dp"), lax.axis_index("tensor")
    c = lax.rem(dp, NC)
    z = lax.rem(lax.div(dp, NC), NZ)
    y = lax.div(dp, NC * NZ)
    return x, y, z, c


def device(x, y, z, c):
    return ((y * NZ + z) * NC + c, x)


def parts_of(value, n):
    out = []
    for _ in range(n):
        part = value.astype(BF16)
        out.append(part)
        value = value - part.astype(F32)
    return out


def orthonormal_rows(pt):
    rank = pt.shape[0]
    gram = [
        jnp.broadcast_to(jnp.sum(pt * pt[k : k + 1], axis=1, keepdims=True), pt.shape)
        for k in range(rank)
    ]
    rows = []
    for k in range(rank):
        pivot = gram[k][k : k + 1]
        root = lax.rsqrt(pivot)
        root = root * (1.5 - 0.5 * pivot * root * root)
        factor = gram[k] * root
        basis = pt[k : k + 1] * root
        rows.append(basis)
        pt = pt - factor * basis
        for j in range(k + 1, rank):
            gram[j] = gram[j] - factor * factor[j : j + 1]
    return jnp.concatenate(rows, axis=0)


def reduce_kernel(
    g_hbm, e_hbm, q_hbm, pt_out, qn, ge,
    qprev, psend, pz, pxy, msend, mrecv, mstack, hs, yrecv, zs, zrecv,
    load_sem, pz_sem, pxy_sem, m_sem, y_sem, z_sem, az_sem, ay_sem, ac_sem, al_sem,
):
    x, y, z, c = position()
    cols = q_hbm.shape[1]
    rows = g_hbm.shape[1]
    rank = q_hbm.shape[0]
    half = rank // NC
    span = cols // NC
    group = span // NZ
    unit = group // 2
    pending = []

    def send(src, dst, sems, index, to):
        copy = pltpu.make_async_remote_copy(
            src_ref=src, dst_ref=dst, send_sem=sems.at[(0,) + index], recv_sem=sems.at[(1,) + index],
            device_id=to, device_id_type=MESH,
        )
        copy.start()
        pending.append(copy)
        return copy

    def drain():
        for copy in pending:
            copy.wait_send()
        pending.clear()

    def peer(dx=0, dy=0, dz=0, dc=0):
        return device(
            lax.rem(x + dx, NX) if dx else x, lax.rem(y + dy, NY) if dy else y,
            lax.rem(z + dz, NZ) if dz else z, 1 - c if dc else c,
        )

    wide = cols // LOADS
    loads = []
    for k in range(LOADS):
        s = pl.ds(k * wide, wide)
        batch = [
            pltpu.make_async_copy(q_hbm.at[:, s], qprev.at[:, s], load_sem.at[k, 0]),
            pltpu.make_async_copy(g_hbm.at[0, :, s], ge.at[pl.ds(0, rows), s], load_sem.at[k, 1]),
            pltpu.make_async_copy(e_hbm.at[0, :, s], ge.at[pl.ds(rows, rows), s], load_sem.at[k, 2]),
        ]
        for copy in batch:
            copy.start()
        loads.append(batch)

    offsets = [(0, 0, dz, dc) for dz in range(NZ) for dc in range(NC)]
    offsets += [(dx, dy, 0, dc) for dx in range(NX) for dy in range(NY) for dc in range(NC)]
    offsets += [(0, dy, dz, 0) for dy in range(NY) for dz in DIRECT]
    offsets = [o for o in dict.fromkeys(offsets) if o != (0, 0, 0, 0)]
    barrier = pltpu.get_barrier_semaphore()
    for o in offsets:
        pl.semaphore_signal(barrier, inc=1, device_id=peer(*o), device_id_type=MESH)

    total = jnp.zeros((3 * rank, rows), F32)
    for k in range(LOADS):
        for copy in loads[k]:
            copy.wait()
        s = pl.ds(k * wide, wide)
        stack = jnp.concatenate(parts_of(qprev[:, s], 3), axis=0)
        for start in (0, rows):
            part = ge[pl.ds(start, rows), s]
            total += lax.dot_general(stack, part, (((1,), (1,)), ((), ())), preferred_element_type=F32)
    mine = total[:rank] + total[rank : 2 * rank] + total[2 * rank :]

    pl.semaphore_wait(barrier, len(offsets))

    psend[0] = mine[:half]
    psend[1] = mine[half:]
    slot = z * NC + c
    copies = []
    for d in FAR + [0]:
        if d:
            copies.append(send(psend.at[c], pz.at[slot], pz_sem, (d, 0), peer(dz=d)))
        copies.append(send(psend.at[1 - c], pz.at[slot], pz_sem, (d, 1), peer(dz=d, dc=1)))
    pz[slot] = psend[c]

    m_copies = []
    for k in range(NZ):
        s = pl.ds(pl.multiple_of((1 - c) * span + k * group, 128), group)
        msend[k] = ge[pl.ds(0, rows), s].astype(F32) + ge[pl.ds(rows, rows), s].astype(F32)
        m_copies.append(send(msend.at[k], mrecv.at[k], m_sem, (k,), peer(dc=1)))

    for copy in copies:
        copy.wait_recv()
    mine = pz[0]
    for k in range(1, NZ * NC):
        mine = mine + pz[k]

    psend[2] = mine
    slot = y * NX + x
    order = sorted(
        [(dx, dy) for dx in range(NX) for dy in range(NY)],
        key=lambda d: -(min(d[0], NX - d[0]) + min(d[1], NY - d[1])),
    )
    copies = []
    for dx, dy in order:
        if (dx, dy) != (0, 0):
            copies.append(send(psend.at[2], pxy.at[slot, c], pxy_sem, (dx, dy, 0), peer(dx, dy)))
        copies.append(send(psend.at[2], pxy.at[slot, c], pxy_sem, (dx, dy, 1), peer(dx, dy, dc=1)))
    pxy[slot, c] = mine

    for k in range(NZ):
        m_copies[k].wait_recv()
        s = pl.ds(pl.multiple_of(c * span + k * group, 128), group)
        both = ge[pl.ds(0, rows), s].astype(F32) + ge[pl.ds(rows, rows), s].astype(F32) + mrecv[k]
        for i, part in enumerate(parts_of(both, 3)):
            mstack[k, pl.ds(i * rows, rows)] = part

    drain()
    for copy in copies:
        copy.wait_recv()
    mine = pxy[0]
    for k in range(1, NX * NY):
        mine = mine + pxy[k]

    basis = orthonormal_rows(mine.reshape(rank, rows))
    pt_out[...] = basis
    stack = jnp.concatenate(parts_of(basis, 3), axis=0)
    stack = jnp.concatenate([stack] * 3, axis=1)

    order = FAR + [0]
    y_copies = {}
    for d in order:
        three = jnp.dot(stack, mstack[lax.rem(z + d, NZ)], preferred_element_type=F32)
        local = three[:rank] + three[rank : 2 * rank] + three[2 * rank :]
        for k in range(NY):
            hs[d, k] = local[k // 2 * half : (k // 2 + 1) * half, k % 2 * unit : (k % 2 + 1) * unit]
        y_copies[d] = [
            send(hs.at[d, lax.rem(y + dy, NY)], yrecv.at[d, dy], y_sem, (d, dy), peer(dy=dy)) for dy in DYS
        ]
    z_copies = []
    for d in order:
        for copy in y_copies[d]:
            copy.wait_recv()
        value = hs[d, y] + yrecv[d, 1] + yrecv[d, 2] + yrecv[d, 3]
        if d:
            zs[d] = value
            z_copies.append(send(zs.at[d], zrecv.at[d], z_sem, (d,), peer(dz=d)))
    drain()
    for copy in z_copies:
        copy.wait_recv()
    for d in range(1, NZ):
        value = value + zrecv[d]
    value = value * (1.0 / (NY * NZ * NC))

    def place(ty, tz):
        start = c * span + tz * group + lax.rem(ty, 2) * unit
        return qn.at[lax.div(ty, 2), :, pl.ds(pl.multiple_of(start, 128), unit)]

    def forward(d):
        start = c * span + lax.rem(z + NZ - d, NZ) * group
        ref = qn.at[:, :, pl.ds(pl.multiple_of(start, 128), group)]
        c_copies.append(send(ref, ref, ac_sem, (d,), peer(dc=1)))

    own = place(y, z)
    own[...] = value
    c_copies, y_copies, z_copies = [], {}, {}
    for d in STAGED:
        z_copies[d] = send(own, own, az_sem, (d,), peer(dz=d))
    for d in DIRECT:
        for dy in (2, 1, 3, 0):
            if d or dy:
                y_copies[d, dy] = send(own, own, ay_sem, (d, dy), peer(dy=dy, dz=d))
    for d in STAGED[::-1]:
        z_copies[d].wait_recv()
        ref = place(y, lax.rem(z + NZ - d, NZ))
        for dy in DYS:
            y_copies[d, dy] = send(ref, ref, ay_sem, (d, dy), peer(dy=dy))
            if d == LAST:
                c_copies.append(send(ref, ref, al_sem, (dy,), peer(dy=dy, dc=1)))
        if d == LAST:
            c_copies.append(send(ref, ref, al_sem, (0,), peer(dc=1)))
    for d in DIRECT[::-1] + STAGED[::-1]:
        for dy in (0, 1, 3, 2):
            if (d, dy) in y_copies:
                y_copies[d, dy].wait_recv()
        if d != LAST:
            forward(d)
    drain()
    for copy in c_copies:
        copy.wait_recv()


def residual_kernel(pt_ref, q_ref, ge, pt_out, q_out, r_out, held, sem, out_sem):
    rows, cols = held.shape
    rank = pt_ref.shape[0]
    block = cols // NZ
    copies = [
        pltpu.make_async_copy(q_ref, q_out, out_sem.at[0]),
        pltpu.make_async_copy(pt_ref, pt_out, out_sem.at[1]),
    ]
    for copy in copies:
        copy.start()
    p1, p2 = parts_of(pt_ref[...].T, 2)
    stack = jnp.concatenate([p1, p1, p2, p2], axis=1)
    for k in range(NZ):
        s = pl.ds(k * block, block)
        q1, q2 = parts_of(q_ref[:, :, s].reshape(rank, block), 2)
        update = jnp.dot(stack, jnp.concatenate([q1, q2, q1, q2], axis=0), preferred_element_type=F32)
        merged = ge[pl.ds(0, rows), s].astype(F32) + ge[pl.ds(rows, rows), s].astype(F32)
        held[:, s] = (merged - update).astype(BF16)
        copy = pltpu.make_async_copy(held.at[:, s], r_out.at[0, :, s], sem.at[k])
        copy.start()
        copies.append(copy)
    for copy in copies:
        copy.wait()


def shards(gradient, error_buffer, q_prev):
    _, rows, cols = gradient.shape
    rank = q_prev.shape[0]
    half = rank // NC
    unit = cols // (NY * NZ)
    group = cols // NC // NZ
    dma = pltpu.SemaphoreType.DMA
    vmem = pltpu.VMEM
    anywhere = pl.BlockSpec(memory_space=pl.ANY)
    inside = pl.BlockSpec(memory_space=pltpu.VMEM)
    pt, qn, ge = pl.pallas_call(
        reduce_kernel,
        out_shape=(
            vmem((rank, rows), F32),
            vmem((NC, half, cols), F32),
            vmem((2 * rows, cols), BF16),
        ),
        in_specs=[anywhere] * 3,
        out_specs=(inside,) * 3,
        scratch_shapes=[
            vmem((rank, cols), F32),
            vmem((3, half, rows), F32),
            vmem((NZ * NC, half, rows), F32),
            vmem((NX * NY, NC, half, rows), F32),
            vmem((NZ, rows, group), F32),
            vmem((NZ, rows, group), F32),
            vmem((NZ, 3 * rows, group), BF16),
            vmem((NZ, NY, half, unit), F32),
            vmem((NZ, NY, half, unit), F32),
            vmem((NZ, half, unit), F32),
            vmem((NZ, half, unit), F32),
            dma((LOADS, 3)),
            dma((2, NZ, NC)),
            dma((2, NX, NY, NC)),
            dma((2, NZ)),
            dma((2, NZ, NY)),
            dma((2, NZ)),
            dma((2, NZ)),
            dma((2, NZ, NY)),
            dma((2, NZ)),
            dma((2, NY)),
        ],
        compiler_params=pltpu.CompilerParams(
            collective_id=0, has_side_effects=True, vmem_limit_bytes=32 * 1024 * 1024
        ),
        cost_estimate=pl.CostEstimate(flops=2 * 10**8, bytes_accessed=8 * 10**6, transcendentals=0),
        name="reduce_factors",
    )(*[pltpu.with_memory_space_constraint(v, pltpu.HBM) for v in (gradient, error_buffer, q_prev)])

    pt, q_new, residual = pl.pallas_call(
        residual_kernel,
        out_shape=(
            jax.ShapeDtypeStruct((rank, rows), F32),
            jax.ShapeDtypeStruct((NC, half, cols), F32),
            jax.ShapeDtypeStruct((1, rows, cols), BF16),
        ),
        in_specs=[inside] * 3,
        out_specs=(anywhere,) * 3,
        scratch_shapes=[vmem((rows, cols), BF16), dma((NZ,)), dma((2,))],
        compiler_params=pltpu.CompilerParams(vmem_limit_bytes=16 * 1024 * 1024),
        cost_estimate=pl.CostEstimate(flops=2 * 10**8, bytes_accessed=11 * 10**6, transcendentals=0),
        name="residual",
    )(pt, qn, ge)
    return pt.T, q_new.reshape(rank, cols), residual


def solution(mesh):
    return jax.shard_map(
        shards,
        mesh=mesh,
        in_specs=(P("dp", None, "tensor"), P("dp", None, "tensor"), P(None, "tensor")),
        out_specs=(P(), P(None, "tensor"), P("dp", None, "tensor")),
        check_vma=False,
    )
```

```python
import functools

import jax
import jax.numpy as jnp
from jax import lax
from jax.experimental import pallas as pl
from jax.experimental.pallas import tpu as pltpu
from jax.sharding import PartitionSpec as P

MESH = pl.DeviceIdType.MESH
F32 = jnp.float32
BF16 = jnp.bfloat16

NX, NY, NZ, NC = 4, 4, 8, 2
FAR = [4, 3, 5, 2, 6, 1, 7]
DIRECT = [2, 6, 1, 7, 0]
STAGED = [4, 3, 5]
DYS = [2, 1, 3]
LAST = 4
LOADS = 6
WRITES = 24


def position():
    dp, x = lax.axis_index("dp"), lax.axis_index("tensor")
    c = lax.rem(dp, NC)
    z = lax.rem(lax.div(dp, NC), NZ)
    y = lax.div(dp, NC * NZ)
    return x, y, z, c


def device(x, y, z, c):
    return ((y * NZ + z) * NC + c, x)


def parts_of(value, n):
    out = []
    for _ in range(n):
        part = value.astype(BF16)
        out.append(part)
        value = value - part.astype(F32)
    return out


def orthonormal_rows(pt):
    rank = pt.shape[0]
    gram = [
        jnp.broadcast_to(jnp.sum(pt * pt[k : k + 1], axis=1, keepdims=True), pt.shape)
        for k in range(rank)
    ]
    rows = []
    for k in range(rank):
        pivot = gram[k][k : k + 1]
        root = lax.rsqrt(pivot)
        root = root * (1.5 - 0.5 * pivot * root * root)
        factor = gram[k] * root
        basis = pt[k : k + 1] * root
        rows.append(basis)
        pt = pt - factor * basis
        for j in range(k + 1, rank):
            gram[j] = gram[j] - factor * factor[j : j + 1]
    return jnp.concatenate(rows, axis=0)


def reduce_kernel(
    g_hbm, e_hbm, q_hbm, pt_out, qn, ge,
    qprev, psend, pz, pxy, msend, mrecv, mstack, hs, yrecv, zs, zrecv,
    load_sem, pz_sem, pxy_sem, m_sem, y_sem, z_sem, az_sem, ay_sem, ac_sem, al_sem,
):
    x, y, z, c = position()
    cols = q_hbm.shape[1]
    rows = g_hbm.shape[1]
    rank = q_hbm.shape[0]
    half = rank // NC
    span = cols // NC
    group = span // NZ
    unit = group // 2
    pending = []

    def send(src, dst, sems, index, to):
        copy = pltpu.make_async_remote_copy(
            src_ref=src, dst_ref=dst, send_sem=sems.at[(0,) + index], recv_sem=sems.at[(1,) + index],
            device_id=to, device_id_type=MESH,
        )
        copy.start()
        pending.append(copy)
        return copy

    def drain():
        for copy in pending:
            copy.wait_send()
        pending.clear()

    def peer(dx=0, dy=0, dz=0, dc=0):
        return device(
            lax.rem(x + dx, NX) if dx else x, lax.rem(y + dy, NY) if dy else y,
            lax.rem(z + dz, NZ) if dz else z, 1 - c if dc else c,
        )

    wide = cols // LOADS
    loads = []
    for k in range(LOADS):
        s = pl.ds(k * wide, wide)
        batch = [
            pltpu.make_async_copy(q_hbm.at[:, s], qprev.at[:, s], load_sem.at[k, 0]),
            pltpu.make_async_copy(g_hbm.at[0, :, s], ge.at[pl.ds(0, rows), s], load_sem.at[k, 1]),
            pltpu.make_async_copy(e_hbm.at[0, :, s], ge.at[pl.ds(rows, rows), s], load_sem.at[k, 2]),
        ]
        for copy in batch:
            copy.start()
        loads.append(batch)

    offsets = [(0, 0, dz, dc) for dz in range(NZ) for dc in range(NC)]
    offsets += [(dx, dy, 0, dc) for dx in range(NX) for dy in range(NY) for dc in range(NC)]
    offsets += [(0, dy, dz, 0) for dy in range(NY) for dz in DIRECT]
    offsets = [o for o in dict.fromkeys(offsets) if o != (0, 0, 0, 0)]
    barrier = pltpu.get_barrier_semaphore()
    for o in offsets:
        pl.semaphore_signal(barrier, inc=1, device_id=peer(*o), device_id_type=MESH)

    total = jnp.zeros((3 * rank, rows), F32)
    for k in range(LOADS):
        for copy in loads[k]:
            copy.wait()
        s = pl.ds(k * wide, wide)
        stack = jnp.concatenate(parts_of(qprev[:, s], 3), axis=0)
        for start in (0, rows):
            part = ge[pl.ds(start, rows), s]
            total += lax.dot_general(stack, part, (((1,), (1,)), ((), ())), preferred_element_type=F32)
    mine = total[:rank] + total[rank : 2 * rank] + total[2 * rank :]

    pl.semaphore_wait(barrier, len(offsets))

    psend[0] = mine[:half]
    psend[1] = mine[half:]
    slot = z * NC + c
    copies = []
    for d in FAR + [0]:
        if d:
            copies.append(send(psend.at[c], pz.at[slot], pz_sem, (d, 0), peer(dz=d)))
        copies.append(send(psend.at[1 - c], pz.at[slot], pz_sem, (d, 1), peer(dz=d, dc=1)))
    pz[slot] = psend[c]

    m_copies = []
    for k in range(NZ):
        s = pl.ds(pl.multiple_of((1 - c) * span + k * group, 128), group)
        msend[k] = ge[pl.ds(0, rows), s].astype(F32) + ge[pl.ds(rows, rows), s].astype(F32)
        m_copies.append(send(msend.at[k], mrecv.at[k], m_sem, (k,), peer(dc=1)))

    for copy in copies:
        copy.wait_recv()
    mine = pz[0]
    for k in range(1, NZ * NC):
        mine = mine + pz[k]

    psend[2] = mine
    slot = y * NX + x
    order = sorted(
        [(dx, dy) for dx in range(NX) for dy in range(NY)],
        key=lambda d: -(min(d[0], NX - d[0]) + min(d[1], NY - d[1])),
    )
    copies = []
    for dx, dy in order:
        if (dx, dy) != (0, 0):
            copies.append(send(psend.at[2], pxy.at[slot, c], pxy_sem, (dx, dy, 0), peer(dx, dy)))
        copies.append(send(psend.at[2], pxy.at[slot, c], pxy_sem, (dx, dy, 1), peer(dx, dy, dc=1)))
    pxy[slot, c] = mine

    for k in range(NZ):
        m_copies[k].wait_recv()
        s = pl.ds(pl.multiple_of(c * span + k * group, 128), group)
        both = ge[pl.ds(0, rows), s].astype(F32) + ge[pl.ds(rows, rows), s].astype(F32) + mrecv[k]
        for i, part in enumerate(parts_of(both, 3)):
            mstack[k, pl.ds(i * rows, rows)] = part

    drain()
    for copy in copies:
        copy.wait_recv()
    mine = pxy[0]
    for k in range(1, NX * NY):
        mine = mine + pxy[k]

    basis = orthonormal_rows(mine.reshape(rank, rows))
    pt_out[...] = basis
    stack = jnp.concatenate(parts_of(basis, 3), axis=0)
    stack = jnp.concatenate([stack] * 3, axis=1)

    order = FAR + [0]
    y_copies = {}
    for d in order:
        three = jnp.dot(stack, mstack[lax.rem(z + d, NZ)], preferred_element_type=F32)
        local = three[:rank] + three[rank : 2 * rank] + three[2 * rank :]
        for k in range(NY):
            hs[d, k] = local[k // 2 * half : (k // 2 + 1) * half, k % 2 * unit : (k % 2 + 1) * unit]
        y_copies[d] = [
            send(hs.at[d, lax.rem(y + dy, NY)], yrecv.at[d, dy], y_sem, (d, dy), peer(dy=dy)) for dy in DYS
        ]
    z_copies = []
    for d in order:
        for copy in y_copies[d]:
            copy.wait_recv()
        value = hs[d, y] + yrecv[d, 1] + yrecv[d, 2] + yrecv[d, 3]
        if d:
            zs[d] = value
            z_copies.append(send(zs.at[d], zrecv.at[d], z_sem, (d,), peer(dz=d)))
    drain()
    for copy in z_copies:
        copy.wait_recv()
    for d in range(1, NZ):
        value = value + zrecv[d]
    value = value * (1.0 / (NY * NZ * NC))

    def place(ty, tz):
        start = c * span + tz * group + lax.rem(ty, 2) * unit
        return qn.at[lax.div(ty, 2), :, pl.ds(pl.multiple_of(start, 128), unit)]

    def forward(d):
        start = c * span + lax.rem(z + NZ - d, NZ) * group
        ref = qn.at[:, :, pl.ds(pl.multiple_of(start, 128), group)]
        c_copies.append(send(ref, ref, ac_sem, (d,), peer(dc=1)))

    own = place(y, z)
    own[...] = value
    c_copies, y_copies, z_copies = [], {}, {}
    for d in STAGED:
        z_copies[d] = send(own, own, az_sem, (d,), peer(dz=d))
    direct = [(d, dy) for d in DIRECT for dy in range(NY) if d or dy]
    for d, dy in sorted(direct, key=lambda o: -min(o[0], NZ - o[0]) - min(o[1], NY - o[1])):
        y_copies[d, dy] = send(own, own, ay_sem, (d, dy), peer(dy=dy, dz=d))
    for d in STAGED[::-1]:
        z_copies[d].wait_recv()
        ref = place(y, lax.rem(z + NZ - d, NZ))
        for dy in DYS:
            y_copies[d, dy] = send(ref, ref, ay_sem, (d, dy), peer(dy=dy))
            if d == LAST:
                c_copies.append(send(ref, ref, al_sem, (dy,), peer(dy=dy, dc=1)))
        if d == LAST:
            c_copies.append(send(ref, ref, al_sem, (0,), peer(dc=1)))
    for d in DIRECT[::-1] + STAGED[::-1]:
        for dy in (0, 1, 3, 2):
            if (d, dy) in y_copies:
                y_copies[d, dy].wait_recv()
        if d != LAST:
            forward(d)
    drain()
    for copy in c_copies:
        copy.wait_recv()


def residual_kernel(pt_ref, q_ref, ge, pt_out, q_out, r_out, held, sem, out_sem):
    rows, cols = held.shape
    rank = pt_ref.shape[0]
    block = cols // WRITES
    copies = [
        pltpu.make_async_copy(q_ref, q_out, out_sem.at[0]),
        pltpu.make_async_copy(pt_ref, pt_out, out_sem.at[1]),
    ]
    for copy in copies:
        copy.start()
    p1, p2 = parts_of(pt_ref[...].T, 2)
    stack = jnp.concatenate([p1, p1, p2, p2], axis=1)
    for k in range(WRITES):
        s = pl.ds(k * block, block)
        q1, q2 = parts_of(q_ref[:, :, s].reshape(rank, block), 2)
        update = jnp.dot(stack, jnp.concatenate([q1, q2, q1, q2], axis=0), preferred_element_type=F32)
        merged = ge[pl.ds(0, rows), s].astype(F32) + ge[pl.ds(rows, rows), s].astype(F32)
        held[:, s] = (merged - update).astype(BF16)
        copy = pltpu.make_async_copy(held.at[:, s], r_out.at[0, :, s], sem.at[k])
        copy.start()
        copies.append(copy)
    for copy in copies:
        copy.wait()


def shards(gradient, error_buffer, q_prev):
    _, rows, cols = gradient.shape
    rank = q_prev.shape[0]
    half = rank // NC
    unit = cols // (NY * NZ)
    group = cols // NC // NZ
    dma = pltpu.SemaphoreType.DMA
    vmem = pltpu.VMEM
    anywhere = pl.BlockSpec(memory_space=pl.ANY)
    inside = pl.BlockSpec(memory_space=pltpu.VMEM)
    pt, qn, ge = pl.pallas_call(
        reduce_kernel,
        out_shape=(
            vmem((rank, rows), F32),
            vmem((NC, half, cols), F32),
            vmem((2 * rows, cols), BF16),
        ),
        in_specs=[anywhere] * 3,
        out_specs=(inside,) * 3,
        scratch_shapes=[
            vmem((rank, cols), F32),
            vmem((3, half, rows), F32),
            vmem((NZ * NC, half, rows), F32),
            vmem((NX * NY, NC, half, rows), F32),
            vmem((NZ, rows, group), F32),
            vmem((NZ, rows, group), F32),
            vmem((NZ, 3 * rows, group), BF16),
            vmem((NZ, NY, half, unit), F32),
            vmem((NZ, NY, half, unit), F32),
            vmem((NZ, half, unit), F32),
            vmem((NZ, half, unit), F32),
            dma((LOADS, 3)),
            dma((2, NZ, NC)),
            dma((2, NX, NY, NC)),
            dma((2, NZ)),
            dma((2, NZ, NY)),
            dma((2, NZ)),
            dma((2, NZ)),
            dma((2, NZ, NY)),
            dma((2, NZ)),
            dma((2, NY)),
        ],
        compiler_params=pltpu.CompilerParams(
            collective_id=0, has_side_effects=True, vmem_limit_bytes=32 * 1024 * 1024
        ),
        cost_estimate=pl.CostEstimate(flops=2 * 10**8, bytes_accessed=8 * 10**6, transcendentals=0),
        name="reduce_factors",
    )(*[pltpu.with_memory_space_constraint(v, pltpu.HBM) for v in (gradient, error_buffer, q_prev)])

    pt, q_new, residual = pl.pallas_call(
        residual_kernel,
        out_shape=(
            jax.ShapeDtypeStruct((rank, rows), F32),
            jax.ShapeDtypeStruct((NC, half, cols), F32),
            jax.ShapeDtypeStruct((1, rows, cols), BF16),
        ),
        in_specs=[inside] * 3,
        out_specs=(anywhere,) * 3,
        scratch_shapes=[vmem((rows, cols), BF16), dma((WRITES,)), dma((2,))],
        compiler_params=pltpu.CompilerParams(vmem_limit_bytes=16 * 1024 * 1024),
        cost_estimate=pl.CostEstimate(flops=2 * 10**8, bytes_accessed=11 * 10**6, transcendentals=0),
        name="residual",
    )(pt, qn, ge)
    return pt.T, q_new.reshape(rank, cols), residual


def solution(mesh):
    return jax.shard_map(
        shards,
        mesh=mesh,
        in_specs=(P("dp", None, "tensor"), P("dp", None, "tensor"), P(None, "tensor")),
        out_specs=(P(), P(None, "tensor"), P("dp", None, "tensor")),
        check_vma=False,
    )
```

```python
import functools

import jax
import jax.numpy as jnp
from jax import lax
from jax.experimental import pallas as pl
from jax.experimental.pallas import tpu as pltpu
from jax.sharding import PartitionSpec as P

MESH = pl.DeviceIdType.MESH
F32 = jnp.float32
BF16 = jnp.bfloat16

NX, NY, NZ, NC = 4, 4, 8, 2
FAR = [4, 3, 5, 2, 6, 1, 7]
DIRECT = [2, 6, 1, 7, 0]
STAGED = [4, 3, 5]
DYS = [2, 1, 3]
LAST = 4
LOADS = 6
WRITES = 24


def position():
    dp, x = lax.axis_index("dp"), lax.axis_index("tensor")
    c = lax.rem(dp, NC)
    z = lax.rem(lax.div(dp, NC), NZ)
    y = lax.div(dp, NC * NZ)
    return x, y, z, c


def device(x, y, z, c):
    return ((y * NZ + z) * NC + c, x)


def parts_of(value, n):
    out = []
    for _ in range(n):
        part = value.astype(BF16)
        out.append(part)
        value = value - part.astype(F32)
    return out


def orthonormal_rows(pt):
    rank = pt.shape[0]
    gram = [
        jnp.broadcast_to(jnp.sum(pt * pt[k : k + 1], axis=1, keepdims=True), pt.shape)
        for k in range(rank)
    ]
    rows = []
    for k in range(rank):
        pivot = gram[k][k : k + 1]
        root = lax.rsqrt(pivot)
        root = root * (1.5 - 0.5 * pivot * root * root)
        factor = gram[k] * root
        basis = pt[k : k + 1] * root
        rows.append(basis)
        pt = pt - factor * basis
        for j in range(k + 1, rank):
            gram[j] = gram[j] - factor * factor[j : j + 1]
    return jnp.concatenate(rows, axis=0)


def reduce_kernel(
    g_hbm, e_hbm, q_hbm, pt_out, qn, ge,
    qprev, psend, pz, pxy, msend, mrecv, mstack, hs, yrecv, zs, zrecv,
    load_sem, pz_sem, pxy_sem, m_sem, y_sem, z_sem, az_sem, ay_sem, ac_sem, al_sem,
):
    x, y, z, c = position()
    cols = q_hbm.shape[1]
    rows = g_hbm.shape[1]
    rank = q_hbm.shape[0]
    half = rank // NC
    span = cols // NC
    group = span // NZ
    unit = group // 2
    def send(src, dst, sems, index, to):
        pltpu.make_async_remote_copy(
            src_ref=src, dst_ref=dst, send_sem=sems.at[0], recv_sem=sems.at[1 + index],
            device_id=to, device_id_type=MESH,
        ).start()

    def take(sem, ref):
        pltpu.make_async_copy(ref, ref, sem).wait()

    def units(n):
        return hs.at[pl.ds(0, n // NY)] if n % NY == 0 else hs.at[0, pl.ds(0, n)]

    def peer(dx=0, dy=0, dz=0, dc=0):
        return device(
            lax.rem(x + dx, NX) if dx else x, lax.rem(y + dy, NY) if dy else y,
            lax.rem(z + dz, NZ) if dz else z, 1 - c if dc else c,
        )

    wide = cols // LOADS
    for k in range(LOADS):
        s = pl.ds(k * wide, wide)
        batch = [
            pltpu.make_async_copy(q_hbm.at[:, s], qprev.at[:, s], load_sem.at[k, 0]),
            pltpu.make_async_copy(g_hbm.at[0, :, s], ge.at[pl.ds(0, rows), s], load_sem.at[k, 1]),
            pltpu.make_async_copy(e_hbm.at[0, :, s], ge.at[pl.ds(rows, rows), s], load_sem.at[k, 1]),
        ]
        for copy in batch:
            copy.start()

    offsets = [(0, 0, dz, dc) for dz in range(NZ) for dc in range(NC)]
    offsets += [(dx, dy, 0, dc) for dx in range(NX) for dy in range(NY) for dc in range(NC)]
    offsets += [(0, dy, dz, 0) for dy in range(NY) for dz in DIRECT]
    offsets = [o for o in dict.fromkeys(offsets) if o != (0, 0, 0, 0)]
    barrier = pltpu.get_barrier_semaphore()
    for o in offsets:
        pl.semaphore_signal(barrier, inc=1, device_id=peer(*o), device_id_type=MESH)

    total = jnp.zeros((3 * rank, rows), F32)
    for k in range(LOADS):
        s = pl.ds(k * wide, wide)
        take(load_sem.at[k, 0], qprev.at[:, s])
        take(load_sem.at[k, 1], ge.at[:, s])
        stack = jnp.concatenate(parts_of(qprev[:, s], 3), axis=0)
        for start in (0, rows):
            part = ge[pl.ds(start, rows), s]
            total += lax.dot_general(stack, part, (((1,), (1,)), ((), ())), preferred_element_type=F32)
    mine = total[:rank] + total[rank : 2 * rank] + total[2 * rank :]

    pl.semaphore_wait(barrier, len(offsets))

    psend[0] = mine[:half]
    psend[1] = mine[half:]
    slot = z * NC + c
    for d in FAR + [0]:
        if d:
            send(psend.at[c], pz.at[slot], pz_sem, 0, peer(dz=d))
        send(psend.at[1 - c], pz.at[slot], pz_sem, 0, peer(dz=d, dc=1))
    pz[slot] = psend[c]

    for k in range(NZ):
        s = pl.ds(pl.multiple_of((1 - c) * span + k * group, 128), group)
        msend[k] = ge[pl.ds(0, rows), s].astype(F32) + ge[pl.ds(rows, rows), s].astype(F32)
        send(msend.at[k], mrecv.at[k], m_sem, k // 4, peer(dc=1))

    take(pz_sem.at[1], pz.at[pl.ds(0, NZ * NC - 1)])
    mine = pz[0]
    for k in range(1, NZ * NC):
        mine = mine + pz[k]

    psend[2] = mine
    slot = (y * NX + x) * NC + c
    order = sorted(
        [(dx, dy) for dx in range(NX) for dy in range(NY)],
        key=lambda d: -(min(d[0], NX - d[0]) + min(d[1], NY - d[1])),
    )
    for dx, dy in order:
        if (dx, dy) != (0, 0):
            send(psend.at[2], pxy.at[slot], pxy_sem, 0, peer(dx, dy))
        send(psend.at[2], pxy.at[slot], pxy_sem, 0, peer(dx, dy, dc=1))
    pxy[slot] = mine

    for k in range(NZ):
        if k % 4 == 0:
            take(m_sem.at[1 + k // 4], mrecv.at[pl.ds(k, 4)])
        s = pl.ds(pl.multiple_of(c * span + k * group, 128), group)
        both = ge[pl.ds(0, rows), s].astype(F32) + ge[pl.ds(rows, rows), s].astype(F32) + mrecv[k]
        for i, part in enumerate(parts_of(both, 3)):
            mstack[k, pl.ds(i * rows, rows)] = part

    take(pz_sem.at[0], pz.at[pl.ds(0, NZ * NC - 1)])
    take(pxy_sem.at[0], pxy.at[pl.ds(0, NX * NY * NC - 1)])
    take(m_sem.at[0], msend)
    take(pxy_sem.at[1], pxy.at[pl.ds(0, NX * NY * NC - 1)])
    halves = [pxy[0], pxy[1]]
    for k in range(NC, NX * NY * NC):
        halves[k % NC] = halves[k % NC] + pxy[k]

    basis = orthonormal_rows(jnp.concatenate(halves, axis=0))
    pt_out[...] = basis
    stack = jnp.concatenate(parts_of(basis, 3), axis=0)
    stack = jnp.concatenate([stack] * 3, axis=1)

    order = FAR + [0]
    for d in order:
        three = jnp.dot(stack, mstack[lax.rem(z + d, NZ)], preferred_element_type=F32)
        local = three[:rank] + three[rank : 2 * rank] + three[2 * rank :]
        for k in range(NY):
            hs[d, k] = local[k // 2 * half : (k // 2 + 1) * half, k % 2 * unit : (k % 2 + 1) * unit]
        for dy in DYS:
            send(hs.at[d, lax.rem(y + dy, NY)], yrecv.at[d, dy], y_sem, d, peer(dy=dy))
    for d in order:
        take(y_sem.at[1 + d], yrecv.at[d, pl.ds(1, NY - 1)])
        value = hs[d, y] + yrecv[d, 1] + yrecv[d, 2] + yrecv[d, 3]
        if d:
            zs[d] = value
            send(zs.at[d], zrecv.at[d], z_sem, 0, peer(dz=d))
    take(y_sem.at[0], units(NZ * (NY - 1)))
    take(z_sem.at[0], zs.at[pl.ds(1, NZ - 1)])
    take(z_sem.at[1], zrecv.at[pl.ds(1, NZ - 1)])
    for d in range(1, NZ):
        value = value + zrecv[d]
    value = value * (1.0 / (NY * NZ * NC))

    def place(ty, tz):
        start = c * span + tz * group + lax.rem(ty, 2) * unit
        return qn.at[lax.div(ty, 2), :, pl.ds(pl.multiple_of(start, 128), unit)]

    def forward(d):
        start = c * span + lax.rem(z + NZ - d, NZ) * group
        ref = qn.at[:, :, pl.ds(pl.multiple_of(start, 128), group)]
        send(ref, ref, ac_sem, 0, peer(dc=1))

    own = place(y, z)
    own[...] = value
    for d in STAGED:
        send(own, own, az_sem, STAGED.index(d), peer(dz=d))
    direct = [(d, dy) for d in DIRECT for dy in range(NY) if d or dy]
    for d, dy in sorted(direct, key=lambda o: -min(o[0], NZ - o[0]) - min(o[1], NY - o[1])):
        send(own, own, ay_sem, d, peer(dy=dy, dz=d))
    for d in STAGED[::-1]:
        take(az_sem.at[1 + STAGED.index(d)], units(1))
        ref = place(y, lax.rem(z + NZ - d, NZ))
        for dy in DYS:
            send(ref, ref, ay_sem, d, peer(dy=dy))
            if d == LAST:
                send(ref, ref, al_sem, 0, peer(dy=dy, dc=1))
        if d == LAST:
            send(ref, ref, al_sem, 0, peer(dc=1))
    for d in DIRECT[::-1] + STAGED[::-1]:
        take(ay_sem.at[1 + d], units(NY if d in DIRECT and d else NY - 1))
        if d != LAST:
            forward(d)
    many = qn.at[:, :, pl.ds(0, (NZ - 1) * group)]
    take(az_sem.at[0], units(len(STAGED)))
    take(ay_sem.at[0], units(len(direct) + len(STAGED) * (NY - 1)))
    take(al_sem.at[0], units(NY))
    take(al_sem.at[1], units(NY))
    take(ac_sem.at[1], many)
    take(ac_sem.at[0], many)


def residual_kernel(pt_ref, q_ref, ge, pt_out, q_out, r_out, held, sem, out_sem):
    rows, cols = held.shape
    rank = pt_ref.shape[0]
    block = cols // WRITES
    copies = [
        pltpu.make_async_copy(q_ref, q_out, out_sem.at[0]),
        pltpu.make_async_copy(pt_ref, pt_out, out_sem.at[1]),
    ]
    for copy in copies:
        copy.start()
    p1, p2 = parts_of(pt_ref[...].T, 2)
    stack = jnp.concatenate([p1, p1, p2, p2], axis=1)
    for k in range(WRITES):
        s = pl.ds(k * block, block)
        q1, q2 = parts_of(q_ref[:, :, s].reshape(rank, block), 2)
        update = jnp.dot(stack, jnp.concatenate([q1, q2, q1, q2], axis=0), preferred_element_type=F32)
        merged = ge[pl.ds(0, rows), s].astype(F32) + ge[pl.ds(rows, rows), s].astype(F32)
        held[:, s] = (merged - update).astype(BF16)
        pltpu.make_async_copy(held.at[:, s], r_out.at[0, :, s], sem).start()
    copies.append(pltpu.make_async_copy(held, r_out.at[0], sem))
    for copy in copies:
        copy.wait()


def shards(gradient, error_buffer, q_prev):
    _, rows, cols = gradient.shape
    rank = q_prev.shape[0]
    half = rank // NC
    unit = cols // (NY * NZ)
    group = cols // NC // NZ
    dma = pltpu.SemaphoreType.DMA
    vmem = pltpu.VMEM
    anywhere = pl.BlockSpec(memory_space=pl.ANY)
    inside = pl.BlockSpec(memory_space=pltpu.VMEM)
    pt, qn, ge = pl.pallas_call(
        reduce_kernel,
        out_shape=(
            vmem((rank, rows), F32),
            vmem((NC, half, cols), F32),
            vmem((2 * rows, cols), BF16),
        ),
        in_specs=[anywhere] * 3,
        out_specs=(inside,) * 3,
        scratch_shapes=[
            vmem((rank, cols), F32),
            vmem((3, half, rows), F32),
            vmem((NZ * NC, half, rows), F32),
            vmem((NX * NY * NC, half, rows), F32),
            vmem((NZ, rows, group), F32),
            vmem((NZ, rows, group), F32),
            vmem((NZ, 3 * rows, group), BF16),
            vmem((NZ, NY, half, unit), F32),
            vmem((NZ, NY, half, unit), F32),
            vmem((NZ, half, unit), F32),
            vmem((NZ, half, unit), F32),
            dma((LOADS, 2)),
            dma((2,)),
            dma((2,)),
            dma((3,)),
            dma((1 + NZ,)),
            dma((2,)),
            dma((1 + len(STAGED),)),
            dma((1 + NZ,)),
            dma((2,)),
            dma((2,)),
        ],
        compiler_params=pltpu.CompilerParams(
            collective_id=0, has_side_effects=True, vmem_limit_bytes=32 * 1024 * 1024
        ),
        cost_estimate=pl.CostEstimate(flops=2 * 10**8, bytes_accessed=8 * 10**6, transcendentals=0),
        name="reduce_factors",
    )(*[pltpu.with_memory_space_constraint(v, pltpu.HBM) for v in (gradient, error_buffer, q_prev)])

    pt, q_new, residual = pl.pallas_call(
        residual_kernel,
        out_shape=(
            jax.ShapeDtypeStruct((rank, rows), F32),
            jax.ShapeDtypeStruct((NC, half, cols), F32),
            jax.ShapeDtypeStruct((1, rows, cols), BF16),
        ),
        in_specs=[inside] * 3,
        out_specs=(anywhere,) * 3,
        scratch_shapes=[vmem((rows, cols), BF16), dma(()), dma((2,))],
        compiler_params=pltpu.CompilerParams(vmem_limit_bytes=16 * 1024 * 1024),
        cost_estimate=pl.CostEstimate(flops=2 * 10**8, bytes_accessed=11 * 10**6, transcendentals=0),
        name="residual",
    )(pt, qn, ge)
    return pt.T, q_new.reshape(rank, cols), residual


def solution(mesh):
    return jax.shard_map(
        shards,
        mesh=mesh,
        in_specs=(P("dp", None, "tensor"), P("dp", None, "tensor"), P(None, "tensor")),
        out_specs=(P(), P(None, "tensor"), P("dp", None, "tensor")),
        check_vma=False,
    )
```

```python
import functools

import jax
import jax.numpy as jnp
from jax import lax
from jax.experimental import pallas as pl
from jax.experimental.pallas import tpu as pltpu
from jax.sharding import PartitionSpec as P

MESH = pl.DeviceIdType.MESH
F32 = jnp.float32
BF16 = jnp.bfloat16

NX, NY, NZ, NC = 4, 4, 8, 2
FAR = [4, 3, 5, 2, 6, 1, 7]
DIRECT = [2, 6, 1, 7, 0]
STAGED = [4, 3, 5]
DYS = [2, 1, 3]
LAST = 4
LOADS = 6
WRITES = 24


def position():
    dp, x = lax.axis_index("dp"), lax.axis_index("tensor")
    c = lax.rem(dp, NC)
    z = lax.rem(lax.div(dp, NC), NZ)
    y = lax.div(dp, NC * NZ)
    return x, y, z, c


def device(x, y, z, c):
    return ((y * NZ + z) * NC + c, x)


def parts_of(value, n):
    out = []
    for _ in range(n):
        part = value.astype(BF16)
        out.append(part)
        value = value - part.astype(F32)
    return out


def orthonormal_rows(pt):
    rank = pt.shape[0]
    gram = [
        jnp.broadcast_to(jnp.sum(pt * pt[k : k + 1], axis=1, keepdims=True), pt.shape)
        for k in range(rank)
    ]
    rows = []
    for k in range(rank):
        pivot = gram[k][k : k + 1]
        root = lax.rsqrt(pivot)
        root = root * (1.5 - 0.5 * pivot * root * root)
        factor = gram[k] * root
        basis = pt[k : k + 1] * root
        rows.append(basis)
        pt = pt - factor * basis
        for j in range(k + 1, rank):
            gram[j] = gram[j] - factor * factor[j : j + 1]
    return jnp.concatenate(rows, axis=0)


def reduce_kernel(
    g_hbm, e_hbm, q_hbm, pt_out, qn, ge,
    qprev, psend, pz, pxy, msend, mrecv, mstack, hs, yrecv, zs, zrecv,
    load_sem, pz_sem, pxy_sem, m_sem, y_sem, z_sem, az_sem, ay_sem, ac_sem, al_sem,
):
    x, y, z, c = position()
    cols = q_hbm.shape[1]
    rows = g_hbm.shape[1]
    rank = q_hbm.shape[0]
    half = rank // NC
    span = cols // NC
    group = span // NZ
    unit = group // 2
    def send(src, dst, sems, index, to):
        pltpu.make_async_remote_copy(
            src_ref=src, dst_ref=dst, send_sem=sems.at[0], recv_sem=sems.at[1 + index],
            device_id=to, device_id_type=MESH,
        ).start()

    def take(sem, ref):
        pltpu.make_async_copy(ref, ref, sem).wait()

    def units(n):
        return hs.at[pl.ds(0, n // NY)] if n % NY == 0 else hs.at[0, pl.ds(0, n)]

    def peer(dx=0, dy=0, dz=0, dc=0):
        return device(
            lax.rem(x + dx, NX) if dx else x, lax.rem(y + dy, NY) if dy else y,
            lax.rem(z + dz, NZ) if dz else z, 1 - c if dc else c,
        )

    wide = cols // LOADS
    for k in range(LOADS):
        s = pl.ds(k * wide, wide)
        batch = [
            pltpu.make_async_copy(q_hbm.at[:, s], qprev.at[:, s], load_sem.at[k, 0]),
            pltpu.make_async_copy(g_hbm.at[0, :, s], ge.at[pl.ds(0, rows), s], load_sem.at[k, 1]),
            pltpu.make_async_copy(e_hbm.at[0, :, s], ge.at[pl.ds(rows, rows), s], load_sem.at[k, 1]),
        ]
        for copy in batch:
            copy.start()

    offsets = [(0, 0, dz, dc) for dz in range(NZ) for dc in range(NC)]
    offsets += [(dx, dy, 0, dc) for dx in range(NX) for dy in range(NY) for dc in range(NC)]
    offsets += [(0, dy, dz, 0) for dy in range(NY) for dz in DIRECT]
    offsets = [o for o in dict.fromkeys(offsets) if o != (0, 0, 0, 0)]
    barrier = pltpu.get_barrier_semaphore()
    for o in offsets:
        pl.semaphore_signal(barrier, inc=1, device_id=peer(*o), device_id_type=MESH)

    total = jnp.zeros((3 * rank, rows), F32)
    for k in range(LOADS):
        s = pl.ds(k * wide, wide)
        take(load_sem.at[k, 0], qprev.at[:, s])
        take(load_sem.at[k, 1], ge.at[:, s])
        stack = jnp.concatenate(parts_of(qprev[:, s], 3), axis=0)
        for start in (0, rows):
            part = ge[pl.ds(start, rows), s]
            total += lax.dot_general(stack, part, (((1,), (1,)), ((), ())), preferred_element_type=F32)
    mine = total[:rank] + total[rank : 2 * rank] + total[2 * rank :]

    pl.semaphore_wait(barrier, len(offsets))

    psend[0] = mine[:half]
    psend[1] = mine[half:]
    slot = z * NC + c
    for d in FAR + [0]:
        if d:
            send(psend.at[c], pz.at[slot], pz_sem, 0, peer(dz=d))
        send(psend.at[1 - c], pz.at[slot], pz_sem, 0, peer(dz=d, dc=1))
    pz[slot] = psend[c]

    for k in range(NZ):
        s = pl.ds(pl.multiple_of((1 - c) * span + k * group, 128), group)
        msend[k] = ge[pl.ds(0, rows), s].astype(F32) + ge[pl.ds(rows, rows), s].astype(F32)
        send(msend.at[k], mrecv.at[k], m_sem, k // 4, peer(dc=1))

    take(pz_sem.at[1], pz.at[pl.ds(0, NZ * NC - 1)])
    mine = pz[0]
    for k in range(1, NZ * NC):
        mine = mine + pz[k]

    psend[2] = mine
    slot = (y * NX + x) * NC + c
    order = sorted(
        [(dx, dy) for dx in range(NX) for dy in range(NY)],
        key=lambda d: -(min(d[0], NX - d[0]) + min(d[1], NY - d[1])),
    )
    for dc in range(NC):
        for dx, dy in order:
            if dx or dy or dc:
                send(psend.at[2], pxy.at[slot], pxy_sem, 0, peer(dx, dy, dc=dc))
    pxy[slot] = mine

    for k in range(NZ):
        if k % 4 == 0:
            take(m_sem.at[1 + k // 4], mrecv.at[pl.ds(k, 4)])
        s = pl.ds(pl.multiple_of(c * span + k * group, 128), group)
        both = ge[pl.ds(0, rows), s].astype(F32) + ge[pl.ds(rows, rows), s].astype(F32) + mrecv[k]
        for i, part in enumerate(parts_of(both, 3)):
            mstack[k, pl.ds(i * rows, rows)] = part

    take(pz_sem.at[0], pz.at[pl.ds(0, NZ * NC - 1)])
    take(pxy_sem.at[0], pxy.at[pl.ds(0, NX * NY * NC - 1)])
    take(m_sem.at[0], msend)
    take(pxy_sem.at[1], pxy.at[pl.ds(0, NX * NY * NC - 1)])
    halves = [pxy[0], pxy[1]]
    for k in range(NC, NX * NY * NC):
        halves[k % NC] = halves[k % NC] + pxy[k]

    basis = orthonormal_rows(jnp.concatenate(halves, axis=0))
    pt_out[...] = basis
    stack = jnp.concatenate(parts_of(basis, 3), axis=0)
    stack = jnp.concatenate([stack] * 3, axis=1)

    order = FAR + [0]
    for d in order:
        three = jnp.dot(stack, mstack[lax.rem(z + d, NZ)], preferred_element_type=F32)
        local = three[:rank] + three[rank : 2 * rank] + three[2 * rank :]
        for k in range(NY):
            hs[d, k] = local[k // 2 * half : (k // 2 + 1) * half, k % 2 * unit : (k % 2 + 1) * unit]
        for dy in DYS:
            send(hs.at[d, lax.rem(y + dy, NY)], yrecv.at[d, dy], y_sem, d, peer(dy=dy))
    for d in order:
        take(y_sem.at[1 + d], yrecv.at[d, pl.ds(1, NY - 1)])
        value = hs[d, y] + yrecv[d, 1] + yrecv[d, 2] + yrecv[d, 3]
        if d:
            zs[d] = value
            send(zs.at[d], zrecv.at[d], z_sem, 0, peer(dz=d))
    take(y_sem.at[0], units(NZ * (NY - 1)))
    take(z_sem.at[0], zs.at[pl.ds(1, NZ - 1)])
    take(z_sem.at[1], zrecv.at[pl.ds(1, NZ - 1)])
    for d in range(1, NZ):
        value = value + zrecv[d]
    value = value * (1.0 / (NY * NZ * NC))

    def place(ty, tz):
        start = c * span + tz * group + lax.rem(ty, 2) * unit
        return qn.at[lax.div(ty, 2), :, pl.ds(pl.multiple_of(start, 128), unit)]

    def forward(d):
        start = c * span + lax.rem(z + NZ - d, NZ) * group
        ref = qn.at[:, :, pl.ds(pl.multiple_of(start, 128), group)]
        send(ref, ref, ac_sem, 0, peer(dc=1))

    own = place(y, z)
    own[...] = value
    for d in STAGED:
        send(own, own, az_sem, STAGED.index(d), peer(dz=d))
    direct = [(d, dy) for d in DIRECT for dy in range(NY) if d or dy]
    for d, dy in sorted(direct, key=lambda o: -min(o[0], NZ - o[0]) - min(o[1], NY - o[1])):
        send(own, own, ay_sem, d, peer(dy=dy, dz=d))
    for d in STAGED[::-1]:
        take(az_sem.at[1 + STAGED.index(d)], units(1))
        ref = place(y, lax.rem(z + NZ - d, NZ))
        for dy in DYS:
            send(ref, ref, ay_sem, d, peer(dy=dy))
            if d == LAST:
                send(ref, ref, al_sem, 0, peer(dy=dy, dc=1))
        if d == LAST:
            send(ref, ref, al_sem, 0, peer(dc=1))
    for d in DIRECT[::-1] + STAGED[::-1]:
        take(ay_sem.at[1 + d], units(NY if d in DIRECT and d else NY - 1))
        if d != LAST:
            forward(d)
    many = qn.at[:, :, pl.ds(0, (NZ - 1) * group)]
    take(az_sem.at[0], units(len(STAGED)))
    take(ay_sem.at[0], units(len(direct) + len(STAGED) * (NY - 1)))
    take(al_sem.at[0], units(NY))
    take(al_sem.at[1], units(NY))
    take(ac_sem.at[1], many)
    take(ac_sem.at[0], many)


def residual_kernel(pt_ref, q_ref, ge, pt_out, q_out, r_out, held, sem, out_sem):
    rows, cols = held.shape
    rank = pt_ref.shape[0]
    block = cols // WRITES
    copies = [
        pltpu.make_async_copy(q_ref, q_out, out_sem.at[0]),
        pltpu.make_async_copy(pt_ref, pt_out, out_sem.at[1]),
    ]
    for copy in copies:
        copy.start()
    p1, p2 = parts_of(pt_ref[...].T, 2)
    stack = jnp.concatenate([p1, p1, p2, p2], axis=1)
    for k in range(WRITES):
        s = pl.ds(k * block, block)
        q1, q2 = parts_of(q_ref[:, :, s].reshape(rank, block), 2)
        update = jnp.dot(stack, jnp.concatenate([q1, q2, q1, q2], axis=0), preferred_element_type=F32)
        merged = ge[pl.ds(0, rows), s].astype(F32) + ge[pl.ds(rows, rows), s].astype(F32)
        held[:, s] = (merged - update).astype(BF16)
        pltpu.make_async_copy(held.at[:, s], r_out.at[0, :, s], sem).start()
    copies.append(pltpu.make_async_copy(held, r_out.at[0], sem))
    for copy in copies:
        copy.wait()


def shards(gradient, error_buffer, q_prev):
    _, rows, cols = gradient.shape
    rank = q_prev.shape[0]
    half = rank // NC
    unit = cols // (NY * NZ)
    group = cols // NC // NZ
    dma = pltpu.SemaphoreType.DMA
    vmem = pltpu.VMEM
    anywhere = pl.BlockSpec(memory_space=pl.ANY)
    inside = pl.BlockSpec(memory_space=pltpu.VMEM)
    pt, qn, ge = pl.pallas_call(
        reduce_kernel,
        out_shape=(
            vmem((rank, rows), F32),
            vmem((NC, half, cols), F32),
            vmem((2 * rows, cols), BF16),
        ),
        in_specs=[anywhere] * 3,
        out_specs=(inside,) * 3,
        scratch_shapes=[
            vmem((rank, cols), F32),
            vmem((3, half, rows), F32),
            vmem((NZ * NC, half, rows), F32),
            vmem((NX * NY * NC, half, rows), F32),
            vmem((NZ, rows, group), F32),
            vmem((NZ, rows, group), F32),
            vmem((NZ, 3 * rows, group), BF16),
            vmem((NZ, NY, half, unit), F32),
            vmem((NZ, NY, half, unit), F32),
            vmem((NZ, half, unit), F32),
            vmem((NZ, half, unit), F32),
            dma((LOADS, 2)),
            dma((2,)),
            dma((2,)),
            dma((3,)),
            dma((1 + NZ,)),
            dma((2,)),
            dma((1 + len(STAGED),)),
            dma((1 + NZ,)),
            dma((2,)),
            dma((2,)),
        ],
        compiler_params=pltpu.CompilerParams(
            collective_id=0, has_side_effects=True, vmem_limit_bytes=32 * 1024 * 1024
        ),
        cost_estimate=pl.CostEstimate(flops=2 * 10**8, bytes_accessed=8 * 10**6, transcendentals=0),
        name="reduce_factors",
    )(*[pltpu.with_memory_space_constraint(v, pltpu.HBM) for v in (gradient, error_buffer, q_prev)])

    pt, q_new, residual = pl.pallas_call(
        residual_kernel,
        out_shape=(
            jax.ShapeDtypeStruct((rank, rows), F32),
            jax.ShapeDtypeStruct((NC, half, cols), F32),
            jax.ShapeDtypeStruct((1, rows, cols), BF16),
        ),
        in_specs=[inside] * 3,
        out_specs=(anywhere,) * 3,
        scratch_shapes=[vmem((rows, cols), BF16), dma(()), dma((2,))],
        compiler_params=pltpu.CompilerParams(vmem_limit_bytes=16 * 1024 * 1024),
        cost_estimate=pl.CostEstimate(flops=2 * 10**8, bytes_accessed=11 * 10**6, transcendentals=0),
        name="residual",
    )(pt, qn, ge)
    return pt.T, q_new.reshape(rank, cols), residual


def solution(mesh):
    return jax.shard_map(
        shards,
        mesh=mesh,
        in_specs=(P("dp", None, "tensor"), P("dp", None, "tensor"), P(None, "tensor")),
        out_specs=(P(), P(None, "tensor"), P("dp", None, "tensor")),
        check_vma=False,
    )
```
